128 devices in a mesh: lat: 8 (over z_lo, x), lon: 16 (over y, z_hi, core).
Axes of the slice: x: 4, y: 4, z: 4 (z_hi: 2, z_lo: 2; z = z_hi * 2 + z_lo), core: 2. Of those that a mesh axis runs over, the one named last changes fastest.
Arguments:
- queries: bfloat16 [1, 64, 256, 1024], P(None, 'lat', 'lon'), may hold values from -180 to 180
- key_vectors: bfloat16 [1, 64, 256, 1024], P(None, 'lat', 'lon'), may hold values from -4.5 to 4.5
- value_vectors: bfloat16 [1, 64, 256, 1024], P(None, 'lat', 'lon'), may hold values from -6 to 6
- cotangent: bfloat16 [1, 64, 256, 1024], P(None, 'lat', 'lon'), may hold values from -6 to 6
- neighbour_lists: int32 [8, 16], replicated, may hold values from 0 to 15, as said below
- list_counts: int32 [8], replicated, may hold values from 3 to 16, as said below
Outputs:
- attended: bfloat16 [1, 64, 256, 1024], P(None, 'lat', 'lon')
- query_grad: bfloat16 [1, 64, 256, 1024], P(None, 'lat', 'lon')
- key_grad: bfloat16 [1, 64, 256, 1024], P(None, 'lat', 'lon')
- value_grad: bfloat16 [1, 64, 256, 1024], P(None, 'lat', 'lon')
The draws below stay inside these ranges and needn't reach their ends.
Inputs may be any that keep to these rules, and one draw needn't show every extreme that they name: `neighbour_lists`: the first list_counts[b] entries of row b are distinct cycle offsets and always include 0, 1 and 15; later entries are padding and name nothing. `list_counts`: band 0 and band 8 - 1 list all 16 offsets.
All inputs are finite; a program needn't handle non-finite values.
Results may differ from the reference program's by a relative error of at most 0.03.
Values may be sent and summed in bfloat16 or wider, within the bound.
No kernel may reach another device: no remote copies, remote signals or barrier semaphores. Data moves between devices by JAX's collectives and lax.ppermute only.
A program may use at most 128 MiB of HBM per device.

```python
import jax
import jax.numpy as jnp
from jax import lax

WIDTH = 1024
HEADS = 16
HEAD_DIM = 64
BATCH = 1
ROWS_DEV = 8
COLS_DEV = 16
BANDS = 8
CYCLE = 16
LAT = 64
LON = 256


def list_draw(key):
    base_key = jax.random.fold_in(key, 7)
    band_ids = jnp.arange(BANDS, dtype=jnp.int32)
    distance = jnp.abs(2 * band_ids + 1 - BANDS)
    half_cycle = (CYCLE - 1) // 2
    widest = jnp.maximum(1, (half_cycle - 1) * (distance + 1) // BANDS)
    radius = 1 + jax.random.randint(jax.random.fold_in(base_key, 1), (BANDS,), 0, widest + 1)
    polar = (band_ids == 0) | (band_ids == BANDS - 1)
    counts = jnp.where(polar, CYCLE, 2 * radius + 1).astype(jnp.int32)
    slots = jnp.arange(CYCLE, dtype=jnp.int32)
    window = jnp.where(slots % 2 == 1, (slots + 1) // 2, (CYCLE - slots // 2) % CYCLE)
    filler = jax.random.randint(jax.random.fold_in(base_key, 2), (BANDS, CYCLE), 0, CYCLE)
    offset_lists = jnp.where(slots[None, :] < counts[:, None], window[None, :], filler)
    return (offset_lists.astype(jnp.int32), counts)


def draw_neighbour_lists(key, part):
    return list_draw(key)[0]


def draw_list_counts(key, part):
    return list_draw(key)[1]


def paired_draw(key):
    shape = (BATCH, LAT, LON, WIDTH)
    base_keys = jnp.clip(jax.random.normal(jax.random.fold_in(key, 102), shape, jnp.float32), -4.0, 4.0)
    base_queries = 2.0 * jnp.clip(jax.random.normal(jax.random.fold_in(key, 101), shape, jnp.float32), -4.0, 4.0)
    queries = base_queries
    key_vectors = base_keys
    return (queries, key_vectors)


def draw_queries(key, part):
    return paired_draw(key)[0].astype(jnp.bfloat16)


def draw_key_vectors(key, part):
    return paired_draw(key)[1].astype(jnp.bfloat16)


def levels(rng, extent, cuts, low, top_value):
    loudness = 1.0
    for dim, parts in cuts:
        heights = jax.random.uniform(jax.random.fold_in(jax.random.fold_in(rng, 6), dim), (parts,), jnp.float32, low / len(cuts), top_value / len(cuts))
        loudness = loudness * jnp.repeat(jnp.exp(heights), extent[dim] // parts).reshape((-1,) + (1,) * (len(extent) - 1 - dim))
    return loudness


def normal_values(key, dims, width, most, shards=(), held_as=jnp.bfloat16):
    entries = width * jax.random.normal(key, dims, jnp.float32)
    if shards:
        entries = entries * levels(key, dims, shards, -0.22, 0.18)
    return jnp.clip(entries, -most, most).astype(held_as)


def setup_inputs(seed: int = 0) -> dict:
    arg_keys = jax.random.split(jax.random.key(seed), 7)
    queries = draw_queries(jax.random.fold_in(arg_keys[6], 71), 0)
    key_vectors = draw_key_vectors(jax.random.fold_in(arg_keys[6], 71), 0)
    value_vectors = normal_values(arg_keys[2], (BATCH, LAT, LON, WIDTH), 1.0, 6.0, ((1, 8), (2, 16)))
    cotangent = normal_values(arg_keys[3], (BATCH, LAT, LON, WIDTH), 1.0, 6.0, ((1, 8), (2, 16)))
    neighbour_lists = draw_neighbour_lists(jax.random.fold_in(arg_keys[6], 71), 0)
    list_counts = draw_list_counts(jax.random.fold_in(arg_keys[6], 71), 0)
    return {"queries": queries, "key_vectors": key_vectors, "value_vectors": value_vectors, "cotangent": cotangent, "neighbour_lists": neighbour_lists, "list_counts": list_counts}


def to_blocks(field):
    shaped = field.reshape(BATCH, BANDS, ROWS_DEV, CYCLE, COLS_DEV, WIDTH)
    return shaped.transpose(0, 1, 3, 2, 4, 5).reshape(BATCH, BANDS, CYCLE, ROWS_DEV * COLS_DEV, WIDTH)


def from_blocks(blocked):
    shaped = blocked.reshape(BATCH, BANDS, CYCLE, ROWS_DEV, COLS_DEV, WIDTH)
    return shaped.transpose(0, 1, 3, 2, 4, 5).reshape(BATCH, LAT, LON, WIDTH)


def reference(queries, key_vectors, value_vectors, cotangent, neighbour_lists, list_counts):
    block_cells = ROWS_DEV * COLS_DEV
    score_scale = HEAD_DIM ** -0.5
    highest_precision = lax.Precision.HIGHEST
    query_blocks = to_blocks(queries)
    key_blocks = to_blocks(key_vectors)
    value_blocks = to_blocks(value_vectors)
    cot_blocks = to_blocks(cotangent)
    offsets = jnp.arange(CYCLE, dtype=jnp.int32)
    live_slots = jnp.arange(neighbour_lists.shape[1], dtype=jnp.int32)[None, :] < list_counts[:, None]
    member = jnp.any((neighbour_lists[:, None, :] == offsets[None, :, None]) & live_slots[:, None, :], axis=2)
    key_count = (CYCLE + 2) * block_cells

    def heads_of(block, count):
        return block.reshape(BATCH, count, HEADS, HEAD_DIM).astype(jnp.float32)

    def one_block(totals, position):
        key_total, value_total = totals
        band_index = position // CYCLE
        sector = position % CYCLE
        lower_band = jnp.maximum(band_index - 1, 0)
        upper_band = jnp.minimum(band_index + 1, BANDS - 1)

        def gather_keys(blocks):
            return jnp.concatenate([blocks[:, band_index], blocks[:, lower_band, sector][:, None], blocks[:, upper_band, sector][:, None]], axis=1)

        key_rows = heads_of(gather_keys(key_blocks), key_count)
        value_rows = heads_of(gather_keys(value_blocks), key_count)
        query_heads = heads_of(query_blocks[:, band_index, sector], block_cells)
        cot_heads = heads_of(cot_blocks[:, band_index, sector], block_cells)
        block_live = jnp.concatenate([member[band_index][(offsets - sector) % CYCLE], jnp.stack([band_index > 0, band_index < BANDS - 1])])
        key_mask = jnp.repeat(block_live, block_cells, total_repeat_length=key_count)
        scores = jnp.einsum("bnhd,bkhd->bhnk", query_heads, key_rows, precision=highest_precision) * score_scale
        scores = jnp.where(key_mask, scores, -jnp.inf)
        highest = jnp.max(scores, axis=-1, keepdims=True)
        logsum = highest + jnp.log(jnp.sum(jnp.exp(scores - highest), axis=-1, keepdims=True))
        weights = jnp.exp(scores - logsum)
        weights_low = lax.optimization_barrier(weights.astype(jnp.bfloat16)).astype(jnp.float32)
        attended = jnp.einsum("bhnk,bkhd->bnhd", weights_low, value_rows, precision=highest_precision).astype(jnp.bfloat16)
        attended_wide = lax.optimization_barrier(attended).astype(jnp.float32)
        product = jnp.einsum("bnhd,bkhd->bhnk", cot_heads, value_rows, precision=highest_precision)
        spread = jnp.einsum("bnhd,bnhd->bhn", cot_heads, attended_wide, precision=highest_precision)
        slopes = lax.optimization_barrier((weights * (product - spread[..., None])).astype(jnp.bfloat16)).astype(jnp.float32)
        query_grad = (score_scale * jnp.einsum("bhnk,bkhd->bnhd", slopes, key_rows, precision=highest_precision)).astype(jnp.bfloat16)
        key_terms = (score_scale * jnp.einsum("bhnk,bnhd->bkhd", slopes, query_heads, precision=highest_precision)).reshape(BATCH, CYCLE + 2, block_cells, WIDTH)
        value_terms = jnp.einsum("bhnk,bnhd->bkhd", weights_low, cot_heads, precision=highest_precision).reshape(BATCH, CYCLE + 2, block_cells, WIDTH)
        key_terms = lax.optimization_barrier(key_terms.astype(jnp.bfloat16)).astype(jnp.float32)
        value_terms = lax.optimization_barrier(value_terms.astype(jnp.bfloat16)).astype(jnp.float32)
        key_total = key_total.at[:, band_index].add(key_terms[:, :CYCLE])
        key_total = key_total.at[:, lower_band, sector].add(key_terms[:, CYCLE])
        key_total = key_total.at[:, upper_band, sector].add(key_terms[:, CYCLE + 1])
        value_total = value_total.at[:, band_index].add(value_terms[:, :CYCLE])
        value_total = value_total.at[:, lower_band, sector].add(value_terms[:, CYCLE])
        value_total = value_total.at[:, upper_band, sector].add(value_terms[:, CYCLE + 1])
        return (key_total, value_total), (attended.reshape(BATCH, block_cells, WIDTH), query_grad.reshape(BATCH, block_cells, WIDTH))

    zeros = jnp.zeros((BATCH, BANDS, CYCLE, block_cells, WIDTH), jnp.float32)
    (key_total, value_total), (attended, query_grad) = lax.scan(one_block, (zeros, zeros), jnp.arange(BANDS * CYCLE, dtype=jnp.int32))

    def arrange(stacked):
        return from_blocks(stacked.reshape(BANDS, CYCLE, BATCH, block_cells, WIDTH).transpose(2, 0, 1, 3, 4))

    return (arrange(attended), arrange(query_grad), from_blocks(key_total.astype(jnp.bfloat16)), from_blocks(value_total.astype(jnp.bfloat16)))
```

```python
import jax
import jax.numpy as jnp
from jax import lax
from jax.experimental import pallas as pl
from jax.experimental.pallas import tpu as pltpu
from jax.sharding import PartitionSpec as P

HEADS = 16
HEAD_DIM = 64
PAIR = 2 * HEAD_DIM
SCALE = HEAD_DIM ** (-0.5)
LOG2E = 1.4426950408889634
MASKED = -1e30
BF16 = jnp.bfloat16
F32 = jnp.float32
NN = (((1,), (0,)), ((), ()))
NT = (((1,), (1,)), ((), ()))
VMEM = pl.BlockSpec(memory_space=pltpu.VMEM)
SMEM = pl.BlockSpec(memory_space=pltpu.SMEM)


def dot(a, b, dims=NN):
    return lax.dot_general(a, b, dims, preferred_element_type=F32)


def pack_pairs(first_ref, second_ref, out_ref):
    for head in range(HEADS):
        lanes = slice(head * HEAD_DIM, (head + 1) * HEAD_DIM)
        out_ref[head] = jnp.concatenate([first_ref[:, lanes], second_ref[:, lanes]], axis=1)


def pack_kv_kernel(key_ref, value_ref, kv_ref):
    pack_pairs(key_ref, value_ref, kv_ref)


def pack_qc_kernel(lists_ref, counts_ref, query_ref, cot_ref, qc_ref, bias_ref):
    pack_pairs(query_ref, cot_ref, qc_ref)
    band = lax.axis_index("lat")
    bands = lists_ref.shape[0]
    slots = lists_ref.shape[1]
    sectors = bias_ref.shape[0] - 2
    shape = (sectors, bias_ref.shape[1])
    cells = shape[1] // sectors
    key_sector = lax.broadcasted_iota(jnp.int32, shape, 0)
    query_sector = lax.broadcasted_iota(jnp.int32, shape, 1) // cells
    offset = key_sector - query_sector
    offset = jnp.where(offset < 0, offset + sectors, offset)
    count = counts_ref[band]
    bias = jnp.full(shape, MASKED, F32)
    for slot in range(slots):
        named = jnp.where(slot < count, lists_ref[band, slot], -1)
        bias = jnp.where(offset == named, 0.0, bias)
    bias_ref[:sectors] = bias
    below = jnp.where(band > 0, 0.0, MASKED).astype(F32)
    above = jnp.where(band < bands - 1, 0.0, MASKED).astype(F32)
    row = lax.broadcasted_iota(jnp.int32, (2, shape[1]), 0)
    bias_ref[sectors:] = jnp.where(row == 0, below, above)


def lane_scale():
    lane = lax.broadcasted_iota(jnp.int32, (1, PAIR), 1)
    return jnp.where(lane < HEAD_DIM, SCALE, 1.0).astype(F32)


def attend_kernel(
    kv_ref, qc_ref, low_ref, high_ref, bias_ref,
    out_ref, grad_ref, low_grad_ref, high_grad_ref,
    kv_t, scores, terms,
):
    sectors, cells, _ = kv_ref.shape
    chunks = sectors // 2
    wide = 2 * cells
    for sector in range(sectors):
        kv_t[:, sector * cells : (sector + 1) * cells] = kv_ref[sector].T
    grad_ref[...] = jnp.zeros_like(grad_ref)
    halves = [slice(a * cells, (a + 1) * cells) for a in range(2)]

    def chunk(t, carry):
        lanes = pl.ds(pl.multiple_of(t * wide, wide), wide)
        qc_t = qc_ref[pl.ds(2 * t, 2)].reshape(wide, PAIR).T
        zeros = jnp.zeros((HEAD_DIM, wide), BF16)
        queries = jnp.concatenate([qc_t[:HEAD_DIM], zeros], axis=0)
        rims = [
            jnp.concatenate([low_ref[2 * t + a], high_ref[2 * t + a]], axis=0) for a in range(2)
        ]
        rims_t = [rim.T for rim in rims]

        def against(block, right):
            if block < chunks:
                return dot(kv_ref[2 * block : 2 * block + 2].reshape(wide, PAIR), right)
            return jnp.concatenate(
                [dot(rims[a], right[:, halves[a]]) for a in range(2)], axis=1
            )

        def gathered(block, part, right):
            rows = slice(block * wide, (block + 1) * wide)
            if block < chunks:
                return dot(kv_t[part, rows], right)
            return jnp.concatenate(
                [dot(rims_t[a][part], right[:, halves[a]]) for a in range(2)], axis=1
            )

        highest = jnp.full((8, wide), -jnp.inf, F32)
        for block in range(chunks + 1):
            rows = slice(block * wide, (block + 1) * wide)
            s = against(block, queries).reshape(2, cells, wide)
            s = s + bias_ref[2 * block : 2 * block + 2, lanes].reshape(2, 1, wide)
            s = s.reshape(wide, wide)
            scores[rows, :] = s
            highest = jnp.maximum(highest, jnp.max(s.reshape(wide // 8, 8, wide), axis=0))
        highest = jnp.max(highest, axis=0, keepdims=True)

        total = jnp.zeros((8, wide), F32)
        out_t = jnp.zeros((HEAD_DIM, wide), F32)
        for block in range(chunks + 1):
            rows = slice(block * wide, (block + 1) * wide)
            p = jnp.exp2((scores[rows, :] - highest) * (SCALE * LOG2E))
            total = total + jnp.sum(p.reshape(wide // 8, 8, wide), axis=0)
            scores[rows, :] = p
            p_low = p.astype(BF16)
            terms[rows, :wide] = p_low
            out_t = out_t + gathered(block, slice(HEAD_DIM, PAIR), p_low)
        inverse = 1.0 / jnp.sum(total, axis=0, keepdims=True)
        out_low = (out_t * inverse).astype(BF16)
        cot_t = (qc_t[HEAD_DIM:].astype(F32) * inverse).astype(BF16)
        spread = jnp.sum(cot_t.astype(F32) * out_low.astype(F32), axis=0, keepdims=True)
        cots = jnp.concatenate([zeros, cot_t], axis=0)
        both = jnp.concatenate([cots, queries], axis=1)

        query_t = jnp.zeros((HEAD_DIM, wide), F32)
        for block in range(chunks + 1):
            rows = slice(block * wide, (block + 1) * wide)
            slopes = (scores[rows, :] * (against(block, cots) - spread)).astype(BF16)
            terms[rows, wide:] = slopes
            query_t = query_t + gathered(block, slice(0, HEAD_DIM), slopes)
            if block < chunks:
                grad = dot(terms[rows, :], both, NT)
                grad_ref[2 * block : 2 * block + 2] += grad.reshape(2, cells, PAIR)
            else:
                for a in range(2):
                    left = jnp.concatenate([terms[rows, halves[a]], slopes[:, halves[a]]], axis=1)
                    right = jnp.concatenate([cots[:, halves[a]], queries[:, halves[a]]], axis=1)
                    grad = dot(left, right, NT) * lane_scale()
                    low_grad_ref[2 * t + a] = grad[:cells].astype(BF16)
                    high_grad_ref[2 * t + a] = grad[cells:].astype(BF16)
        packed = jnp.concatenate([(query_t * SCALE).astype(BF16), out_low], axis=0)
        out_ref[pl.ds(2 * t, 2)] = packed.T.reshape(2, cells, PAIR)
        return carry

    lax.fori_loop(0, chunks, chunk, 0)
    grad_ref[...] = grad_ref[...] * lane_scale().reshape(1, 1, PAIR)


def unpack_kernel(out_ref, grad_ref, attended_ref, query_ref, key_ref, value_ref):
    for head in range(0, HEADS, 2):
        lanes = slice(head * HEAD_DIM, (head + 2) * HEAD_DIM)
        for pair_ref, first_ref, second_ref in (
            (out_ref, query_ref, attended_ref),
            (grad_ref, key_ref, value_ref),
        ):
            one, two = pair_ref[head], pair_ref[head + 1]
            first_ref[:, lanes] = jnp.concatenate([one[:, :HEAD_DIM], two[:, :HEAD_DIM]], axis=1)
            second_ref[:, lanes] = jnp.concatenate([one[:, HEAD_DIM:], two[:, HEAD_DIM:]], axis=1)


def cost(flops, nbytes):
    return pl.CostEstimate(flops=flops, bytes_accessed=nbytes, transcendentals=0)


def per_device(queries, key_vectors, value_vectors, cotangent, neighbour_lists, list_counts):
    _, band_rows, cycle_cols, features = queries.shape
    cells = band_rows * cycle_cols
    sectors = lax.axis_size("lon")
    bands = lax.axis_size("lat")
    flat = (cells, features)
    by_head = jax.ShapeDtypeStruct((HEADS, cells, PAIR), BF16)
    by_sector = jax.ShapeDtypeStruct((sectors, cells, PAIR), BF16)
    key_rows = (sectors + 2) * cells

    kv = pl.pallas_call(
        pack_kv_kernel, out_shape=by_head, in_specs=[VMEM] * 2, out_specs=VMEM,
        cost_estimate=cost(0, 1 << 20), name="pack_kv",
    )(key_vectors.reshape(flat), value_vectors.reshape(flat))
    qc, bias = pl.pallas_call(
        pack_qc_kernel,
        out_shape=(by_head, jax.ShapeDtypeStruct((sectors + 2, sectors * cells), F32)),
        in_specs=[SMEM] * 2 + [VMEM] * 2, out_specs=(VMEM,) * 2,
        cost_estimate=cost(0, 1 << 20), name="pack_qc",
    )(neighbour_lists, list_counts, queries.reshape(flat), cotangent.reshape(flat))

    kv = lax.all_to_all(kv, "lon", 0, 0, tiled=True)
    up = [(band, (band + 1) % bands) for band in range(bands)]
    down = [(target, source) for source, target in up]
    low = lax.ppermute(kv, "lat", up)
    high = lax.ppermute(kv, "lat", down)
    qc = lax.all_to_all(qc, "lon", 0, 0, tiled=True)

    out, grad, low_grad, high_grad = pl.pallas_call(
        attend_kernel,
        out_shape=(by_sector, jax.ShapeDtypeStruct(by_sector.shape, F32), by_sector, by_sector),
        in_specs=[VMEM] * 5, out_specs=(VMEM,) * 4,
        scratch_shapes=[
            pltpu.VMEM((PAIR, sectors * cells), BF16),
            pltpu.VMEM((key_rows, 2 * cells), F32),
            pltpu.VMEM((key_rows, 4 * cells), BF16),
        ],
        compiler_params=pltpu.CompilerParams(vmem_limit_bytes=40 * 1024 * 1024),
        cost_estimate=cost(25 * 10**9, 8 << 20), name="attend",
    )(kv, qc, low, high, bias)

    from_high = lax.ppermute(low_grad, "lat", down)
    from_low = lax.ppermute(high_grad, "lat", up)
    out = lax.all_to_all(out, "lon", 0, 0, tiled=True)
    grad = (grad + from_high.astype(F32) + from_low.astype(F32)).astype(BF16)
    grad = lax.all_to_all(grad, "lon", 0, 0, tiled=True)

    flat_shape = jax.ShapeDtypeStruct(flat, BF16)
    results = pl.pallas_call(
        unpack_kernel, out_shape=(flat_shape,) * 4, in_specs=[VMEM] * 2, out_specs=(VMEM,) * 4,
        cost_estimate=cost(0, 2 << 20), name="unpack",
    )(out, grad)
    return tuple(result.reshape(queries.shape) for result in results)


def solution(mesh):
    blocks = P(None, "lat", "lon", None)
    return jax.shard_map(
        per_device, mesh=mesh, in_specs=(blocks,) * 4 + (P(), P()), out_specs=(blocks,) * 4,
        check_vma=False,
    )
```

```python
import jax
import jax.numpy as jnp
from jax import lax
from jax.experimental import pallas as pl
from jax.experimental.pallas import tpu as pltpu
from jax.sharding import PartitionSpec as P

HEADS = 16
HEAD_DIM = 64
PAIR = 2 * HEAD_DIM
SCALE = HEAD_DIM ** (-0.5)
LOG2E = 1.4426950408889634
MASKED = -1e30
BF16 = jnp.bfloat16
F32 = jnp.float32
NN = (((1,), (0,)), ((), ()))
NT = (((1,), (1,)), ((), ()))
VMEM = pl.BlockSpec(memory_space=pltpu.VMEM)
SMEM = pl.BlockSpec(memory_space=pltpu.SMEM)


def dot(a, b, dims=NN):
    return lax.dot_general(a, b, dims, preferred_element_type=F32)


def pack_pairs(first_ref, second_ref, out_ref, rows):
    for head in range(HEADS):
        lanes = slice(head * HEAD_DIM, (head + 1) * HEAD_DIM)
        out_ref[head, rows] = jnp.concatenate([first_ref[:, lanes], second_ref[:, lanes]], axis=1)


def pack_kernel(
    lists_ref, counts_ref, key_ref, value_ref, query_ref, cot_ref, packed_ref, bias_ref
):
    cells = key_ref.shape[0]
    pack_pairs(key_ref, value_ref, packed_ref, slice(0, cells))
    pack_pairs(query_ref, cot_ref, packed_ref, slice(cells, 2 * cells))
    band = lax.axis_index("lat")
    bands, slots = lists_ref.shape
    sectors = bias_ref.shape[0] - 2
    shape = (sectors, bias_ref.shape[1])
    key_sector = lax.broadcasted_iota(jnp.int32, shape, 0)
    query_sector = lax.broadcasted_iota(jnp.int32, shape, 1) // cells
    offset = key_sector - query_sector
    offset = jnp.where(offset < 0, offset + sectors, offset)
    count = counts_ref[band]
    bias = jnp.full(shape, MASKED, F32)
    for slot in range(slots):
        named = jnp.where(slot < count, lists_ref[band, slot], -1)
        bias = jnp.where(offset == named, 0.0, bias)
    bias_ref[:sectors] = bias
    below = jnp.where(band > 0, 0.0, MASKED).astype(F32)
    above = jnp.where(band < bands - 1, 0.0, MASKED).astype(F32)
    row = lax.broadcasted_iota(jnp.int32, (2, shape[1]), 0)
    bias_ref[sectors:] = jnp.where(row == 0, below, above)


def lane_scale():
    lane = lax.broadcasted_iota(jnp.int32, (1, PAIR), 1)
    return jnp.where(lane < HEAD_DIM, SCALE, 1.0).astype(F32)


def fold_rows(values, combine):
    return combine(values.reshape(values.shape[0] // 8, 8, values.shape[1]), axis=0)


def forward_kernel(x_ref, bias_ref, weights_ref, highest_ref, total_ref, out_ref, kv_t_ref, scores):
    sectors, both, _ = x_ref.shape
    cells = both // 2
    chunks = sectors // 2
    wide = 2 * cells
    t = pl.program_id(0)

    @pl.when(t == 0)
    def _():
        for sector in range(sectors):
            kv_t_ref[:, sector * cells : (sector + 1) * cells] = x_ref[sector, :cells].T

    lanes = pl.ds(pl.multiple_of(t * wide, wide), wide)
    qc_t = x_ref[pl.ds(2 * t, 2), cells:].reshape(wide, PAIR).T
    queries = jnp.concatenate([qc_t[:HEAD_DIM], jnp.zeros((HEAD_DIM, wide), BF16)], axis=0)
    highest = jnp.full((8, wide), -jnp.inf, F32)
    for block in range(chunks):
        rows = slice(block * wide, (block + 1) * wide)
        s = dot(x_ref[2 * block : 2 * block + 2, :cells].reshape(wide, PAIR), queries)
        s = s.reshape(2, cells, wide)
        s = s + bias_ref[2 * block : 2 * block + 2, lanes].reshape(2, 1, wide)
        s = s.reshape(wide, wide)
        scores[rows, :] = s
        highest = jnp.maximum(highest, fold_rows(s, jnp.max))
    highest = jnp.max(highest, axis=0, keepdims=True)
    total = jnp.zeros((8, wide), F32)
    out_t = jnp.zeros((HEAD_DIM, wide), F32)
    for block in range(chunks):
        rows = slice(block * wide, (block + 1) * wide)
        p = jnp.exp2((scores[rows, :] - highest) * (SCALE * LOG2E))
        total = total + fold_rows(p, jnp.sum)
        p_low = p.astype(BF16)
        weights_ref[0, rows, :] = p_low
        out_t = out_t + dot(kv_t_ref[HEAD_DIM:, rows], p_low)
    highest_ref[0] = highest
    total_ref[0] = jnp.sum(total, axis=0, keepdims=True)
    out_ref[0] = out_t


def rims_kernel(
    x_ref, bias_ref, low_ref, high_ref, highest_ref, total_ref, out_ref,
    attended_ref, cot_ref, spread_ref, query_ref, low_grad_ref, high_grad_ref,
):
    sectors, both, _ = x_ref.shape
    cells = both // 2
    wide = 2 * cells
    t = pl.program_id(0)
    lanes = pl.ds(pl.multiple_of(t * wide, wide), wide)
    qc_t = x_ref[pl.ds(2 * t, 2), cells:].reshape(wide, PAIR).T
    zeros = jnp.zeros((HEAD_DIM, wide), BF16)
    queries = jnp.concatenate([qc_t[:HEAD_DIM], zeros], axis=0)
    halves = [slice(a * cells, (a + 1) * cells) for a in range(2)]
    rims = [jnp.concatenate([low_ref[a], high_ref[a]], axis=0) for a in range(2)]
    rims_t = [rim.T for rim in rims]

    def paired(parts):
        return jnp.concatenate(parts, axis=1)

    s = paired([dot(rims[a], queries[:, halves[a]]) for a in range(2)]).reshape(2, cells, wide)
    s = (s + bias_ref[sectors : sectors + 2, lanes].reshape(2, 1, wide)).reshape(wide, wide)
    own = highest_ref[0]
    highest = jnp.maximum(own, jnp.max(fold_rows(s, jnp.max), axis=0, keepdims=True))
    p = jnp.exp2((s - highest) * (SCALE * LOG2E))
    p_low = p.astype(BF16)
    ratio = jnp.exp2((own - highest) * (SCALE * LOG2E))
    total = ratio * total_ref[0] + jnp.sum(fold_rows(p, jnp.sum), axis=0, keepdims=True)
    inverse = 1.0 / total
    out_t = out_ref[0] * ratio
    out_t = out_t + paired([dot(rims_t[a][HEAD_DIM:], p_low[:, halves[a]]) for a in range(2)])
    attended = (out_t * inverse).astype(BF16)
    attended_ref[0] = attended
    cot_t = qc_t[HEAD_DIM:].astype(F32) * inverse
    own_cot = (cot_t * ratio).astype(BF16)
    cot_ref[0] = own_cot
    spread_ref[0] = jnp.sum(own_cot.astype(F32) * attended.astype(F32), axis=0, keepdims=True)
    cot_t = cot_t.astype(BF16)
    spread = jnp.sum(cot_t.astype(F32) * attended.astype(F32), axis=0, keepdims=True)
    cots = jnp.concatenate([zeros, cot_t], axis=0)
    product = paired([dot(rims[a], cots[:, halves[a]]) for a in range(2)])
    slopes = (p * (product - spread)).astype(BF16)
    query_ref[0] = paired([dot(rims_t[a][:HEAD_DIM], slopes[:, halves[a]]) for a in range(2)])
    for a in range(2):
        left = paired([p_low[:, halves[a]], slopes[:, halves[a]]])
        right = paired([cots[:, halves[a]], queries[:, halves[a]]])
        grad = dot(left, right, NT) * lane_scale()
        low_grad_ref[a] = grad[:cells].astype(BF16)
        high_grad_ref[a] = grad[cells:].astype(BF16)


def backward_kernel(
    x_ref, kv_t_ref, weights_ref, attended_ref, cot_ref, spread_ref, query_ref, out_ref, grad_ref
):
    sectors, both, _ = x_ref.shape
    cells = both // 2
    chunks = sectors // 2
    wide = 2 * cells
    t = pl.program_id(0)

    @pl.when(t == 0)
    def _():
        grad_ref[...] = jnp.zeros_like(grad_ref)

    queries = x_ref[pl.ds(2 * t, 2), cells:].reshape(wide, PAIR).T[:HEAD_DIM]
    zeros = jnp.zeros((HEAD_DIM, wide), BF16)
    queries = jnp.concatenate([queries, zeros], axis=0)
    cots = jnp.concatenate([zeros, cot_ref[0]], axis=0)
    right = jnp.concatenate([cots, queries], axis=1)
    spread = spread_ref[0]
    query_t = query_ref[0]
    for block in range(chunks):
        rows = slice(block * wide, (block + 1) * wide)
        product = dot(x_ref[2 * block : 2 * block + 2, :cells].reshape(wide, PAIR), cots)
        weights = weights_ref[0, rows, :]
        slopes = (weights.astype(F32) * (product - spread)).astype(BF16)
        query_t = query_t + dot(kv_t_ref[:HEAD_DIM, rows], slopes)
        grad = dot(jnp.concatenate([weights, slopes], axis=1), right, NT)
        grad_ref[2 * block : 2 * block + 2] += grad.reshape(2, cells, PAIR)
    packed = jnp.concatenate([(query_t * SCALE).astype(BF16), attended_ref[0]], axis=0)
    out_ref[...] = packed.T.reshape(2, cells, PAIR)

    @pl.when(t == chunks - 1)
    def _():
        grad_ref[...] = grad_ref[...] * lane_scale().reshape(1, 1, PAIR)


def merge_kernel(out_ref, grad_ref, from_low_ref, from_high_ref, merged_ref):
    cells = out_ref.shape[1]
    merged_ref[:, :cells] = out_ref[...]
    grad = grad_ref[...] + from_low_ref[...].astype(F32) + from_high_ref[...].astype(F32)
    merged_ref[:, cells:] = grad.astype(BF16)


def unpack_kernel(merged_ref, attended_ref, query_ref, key_ref, value_ref):
    cells = attended_ref.shape[0]
    for head in range(0, HEADS, 2):
        lanes = slice(head * HEAD_DIM, (head + 2) * HEAD_DIM)
        for rows, first_ref, second_ref in (
            (slice(0, cells), query_ref, attended_ref),
            (slice(cells, 2 * cells), key_ref, value_ref),
        ):
            one, two = merged_ref[head, rows], merged_ref[head + 1, rows]
            first_ref[:, lanes] = jnp.concatenate([one[:, :HEAD_DIM], two[:, :HEAD_DIM]], axis=1)
            second_ref[:, lanes] = jnp.concatenate([one[:, HEAD_DIM:], two[:, HEAD_DIM:]], axis=1)


def cost(flops, nbytes):
    return pl.CostEstimate(flops=flops, bytes_accessed=nbytes, transcendentals=0)


def whole(*shape):
    return pl.BlockSpec(shape, lambda t: (0,) * len(shape))


def step(*shape):
    return pl.BlockSpec(shape, lambda t: (t,) + (0,) * (len(shape) - 1))


def per_device(queries, key_vectors, value_vectors, cotangent, neighbour_lists, list_counts):
    _, band_rows, cycle_cols, features = queries.shape
    cells = band_rows * cycle_cols
    sectors = lax.axis_size("lon")
    bands = lax.axis_size("lat")
    chunks = sectors // 2
    wide = 2 * cells
    keys = sectors * cells
    flat = (cells, features)
    params = pltpu.CompilerParams(vmem_limit_bytes=32 * 1024 * 1024)
    small = pltpu.CompilerParams(vmem_limit_bytes=16 * 1024 * 1024)
    struct = jax.ShapeDtypeStruct
    paired = struct((sectors, cells, PAIR), BF16)

    packed, bias = pl.pallas_call(
        pack_kernel,
        out_shape=(struct((HEADS, wide, PAIR), BF16), struct((sectors + 2, keys), F32)),
        in_specs=[SMEM] * 2 + [VMEM] * 4, out_specs=(VMEM,) * 2,
        cost_estimate=cost(0, 2 << 20), name="pack",
    )(
        neighbour_lists, list_counts, key_vectors.reshape(flat), value_vectors.reshape(flat),
        queries.reshape(flat), cotangent.reshape(flat),
    )
    x = lax.all_to_all(packed, "lon", 0, 0, tiled=True)
    kv = x[:, :cells]
    up = [(band, (band + 1) % bands) for band in range(bands)]
    down = [(target, source) for source, target in up]
    low = lax.ppermute(kv, "lat", up)
    high = lax.ppermute(kv, "lat", down)

    x_spec = whole(sectors, wide, PAIR)
    bias_spec = whole(sectors + 2, keys)
    row = step(1, 1, wide)
    tall = step(1, HEAD_DIM, wide)
    two = step(2, cells, PAIR)
    weights_spec = step(1, keys, wide)
    kv_t_spec = whole(PAIR, keys)
    row_shape = struct((chunks, 1, wide), F32)
    tall_shape = struct((chunks, HEAD_DIM, wide), F32)
    tall_low = struct((chunks, HEAD_DIM, wide), BF16)

    weights, highest, total, out_t, kv_t = pl.pallas_call(
        forward_kernel, grid=(chunks,),
        out_shape=(
            struct((chunks, keys, wide), BF16), row_shape, row_shape, tall_shape,
            struct((PAIR, keys), BF16),
        ),
        in_specs=[x_spec, bias_spec], out_specs=(weights_spec, row, row, tall, kv_t_spec),
        scratch_shapes=[pltpu.VMEM((keys, wide), F32)],
        compiler_params=params, cost_estimate=cost(10**10, 10 << 20), name="forward",
    )(x, bias)
    attended, cot, spread, query_t, low_grad, high_grad = pl.pallas_call(
        rims_kernel, grid=(chunks,),
        out_shape=(tall_low, tall_low, row_shape, tall_shape, paired, paired),
        in_specs=[x_spec, bias_spec, two, two, row, row, tall],
        out_specs=(tall, tall, row, tall, two, two),
        compiler_params=params, cost_estimate=cost(4 * 10**9, 4 << 20), name="rims",
    )(x, bias, low, high, highest, total, out_t)
    from_high = lax.ppermute(low_grad, "lat", down)
    from_low = lax.ppermute(high_grad, "lat", up)
    out, grad = pl.pallas_call(
        backward_kernel, grid=(chunks,),
        out_shape=(paired, struct(paired.shape, F32)),
        in_specs=[x_spec, kv_t_spec, weights_spec, tall, tall, row, tall],
        out_specs=(two, whole(sectors, cells, PAIR)),
        compiler_params=params, cost_estimate=cost(15 * 10**9, 12 << 20), name="backward",
    )(x, kv_t, weights, attended, cot, spread, query_t)
    merged = pl.pallas_call(
        merge_kernel, out_shape=struct((sectors, wide, PAIR), BF16),
        in_specs=[VMEM] * 4, out_specs=VMEM, compiler_params=small, cost_estimate=cost(0, 4 << 20), name="merge",
    )(out, grad, from_low, from_high)
    merged = lax.all_to_all(merged, "lon", 0, 0, tiled=True)
    results = pl.pallas_call(
        unpack_kernel, out_shape=(struct(flat, BF16),) * 4, in_specs=[VMEM], out_specs=(VMEM,) * 4,
        compiler_params=small, cost_estimate=cost(0, 2 << 20), name="unpack",
    )(merged)
    return tuple(result.reshape(queries.shape) for result in results)


def solution(mesh):
    blocks = P(None, "lat", "lon", None)
    return jax.shard_map(
        per_device, mesh=mesh, in_specs=(blocks,) * 4 + (P(), P()), out_specs=(blocks,) * 4,
        check_vma=False,
    )
```

```python
import jax
import jax.numpy as jnp
from jax import lax
from jax.experimental import pallas as pl
from jax.experimental.pallas import tpu as pltpu
from jax.sharding import PartitionSpec as P

HEADS = 16
HEAD_DIM = 64
PAIR = 2 * HEAD_DIM
SCALE = HEAD_DIM ** (-0.5)
LOG2E = 1.4426950408889634
MASKED = -1e30
CHUNK = 4
BF16 = jnp.bfloat16
F32 = jnp.float32
NN = (((1,), (0,)), ((), ()))
NT = (((1,), (1,)), ((), ()))
VMEM = pl.BlockSpec(memory_space=pltpu.VMEM)
SMEM = pl.BlockSpec(memory_space=pltpu.SMEM)


def dot(a, b, dims=NN):
    return lax.dot_general(a, b, dims, preferred_element_type=F32)


def pack_pairs(first_ref, second_ref, out_ref, rows):
    for head in range(HEADS):
        lanes = slice(head * HEAD_DIM, (head + 1) * HEAD_DIM)
        out_ref[head, rows] = jnp.concatenate([first_ref[:, lanes], second_ref[:, lanes]], axis=1)


def pack_kernel(
    lists_ref, counts_ref, key_ref, value_ref, query_ref, cot_ref, packed_ref, bias_ref
):
    cells = key_ref.shape[0]
    pack_pairs(key_ref, value_ref, packed_ref, slice(0, cells))
    pack_pairs(query_ref, cot_ref, packed_ref, slice(cells, 2 * cells))
    band = lax.axis_index("lat")
    bands, slots = lists_ref.shape
    sectors = bias_ref.shape[0] - 2
    shape = (sectors, bias_ref.shape[1])
    key_sector = lax.broadcasted_iota(jnp.int32, shape, 0)
    query_sector = lax.broadcasted_iota(jnp.int32, shape, 1) // cells
    offset = key_sector - query_sector
    offset = jnp.where(offset < 0, offset + sectors, offset)
    count = counts_ref[band]
    bias = jnp.full(shape, MASKED, F32)
    for slot in range(slots):
        named = jnp.where(slot < count, lists_ref[band, slot], -1)
        bias = jnp.where(offset == named, 0.0, bias)
    bias_ref[:sectors] = bias
    below = jnp.where(band > 0, 0.0, MASKED).astype(F32)
    above = jnp.where(band < bands - 1, 0.0, MASKED).astype(F32)
    row = lax.broadcasted_iota(jnp.int32, (2, shape[1]), 0)
    bias_ref[sectors:] = jnp.where(row == 0, below, above)


def lane_scale():
    lane = lax.broadcasted_iota(jnp.int32, (1, PAIR), 1)
    return jnp.where(lane < HEAD_DIM, SCALE, 1.0).astype(F32)


def fold_rows(values, combine):
    return combine(values.reshape(values.shape[0] // 8, 8, values.shape[1]), axis=0)


def forward_kernel(x_ref, bias_ref, weights_ref, highest_ref, total_ref, out_ref, kv_t_ref, scores):
    sectors, both, _ = x_ref.shape
    cells = both // 2
    chunks, keys, wide = weights_ref.shape
    kv_t_ref[...] = x_ref[:, :cells].reshape(keys, PAIR).T

    def chunk(t, carry):
        lanes = pl.ds(pl.multiple_of(t * wide, wide), wide)
        here = pl.ds(t * (wide // cells), wide // cells)
        queries_t = x_ref[here, cells:].reshape(wide, PAIR).T[:HEAD_DIM]
        queries = jnp.concatenate([queries_t, jnp.zeros((HEAD_DIM, wide), BF16)], axis=0)
        highest = jnp.full((8, wide), -jnp.inf, F32)
        for block in range(0, sectors, 2):
            rows = slice(block * cells, (block + 2) * cells)
            s = dot(x_ref[block : block + 2, :cells].reshape(2 * cells, PAIR), queries)
            s = s.reshape(2, cells, wide) + bias_ref[block : block + 2, lanes].reshape(2, 1, wide)
            s = s.reshape(2 * cells, wide)
            scores[rows, :] = s
            highest = jnp.maximum(highest, fold_rows(s, jnp.max))
        highest = jnp.max(highest, axis=0, keepdims=True)
        total = jnp.zeros((8, wide), F32)
        for block in range(0, sectors, 2):
            rows = slice(block * cells, (block + 2) * cells)
            p = jnp.exp2((scores[rows, :] - highest) * (SCALE * LOG2E))
            total = total + fold_rows(p, jnp.sum)
            weights_ref[t, rows, :] = p.astype(BF16)
        highest_ref[t] = highest
        total_ref[t] = jnp.sum(total, axis=0, keepdims=True)
        out_ref[t] = dot(kv_t_ref[HEAD_DIM:, :], weights_ref[t])
        return carry

    lax.fori_loop(0, chunks, chunk, 0)


def rims_kernel(
    x_ref, bias_ref, low_ref, high_ref, highest_ref, total_ref, out_ref,
    attended_ref, cot_ref, spread_ref, query_ref, low_grad_ref, high_grad_ref,
):
    sectors, both, _ = x_ref.shape
    cells = both // 2
    chunks, _, wide = out_ref.shape
    count = wide // cells
    parts = [slice(a * cells, (a + 1) * cells) for a in range(count)]

    def chunk(t, carry):
        lanes = pl.ds(pl.multiple_of(t * wide, wide), wide)
        first = t * count
        qc_t = x_ref[pl.ds(first, count), cells:].reshape(wide, PAIR).T
        zeros = jnp.zeros((HEAD_DIM, wide), BF16)
        queries = jnp.concatenate([qc_t[:HEAD_DIM], zeros], axis=0)
        rims = [
            jnp.concatenate([low_ref[first + a], high_ref[first + a]], axis=0)
            for a in range(count)
        ]
        rims_t = [rim.T for rim in rims]

        def beside(values):
            return jnp.concatenate(values, axis=1)

        s = beside([dot(rim, queries[:, part]) for rim, part in zip(rims, parts)])
        s = s.reshape(2, cells, wide) + bias_ref[sectors : sectors + 2, lanes].reshape(2, 1, wide)
        s = s.reshape(2 * cells, wide)
        own = highest_ref[t]
        highest = jnp.maximum(own, jnp.max(fold_rows(s, jnp.max), axis=0, keepdims=True))
        p = jnp.exp2((s - highest) * (SCALE * LOG2E))
        p_low = p.astype(BF16)
        ratio = jnp.exp2((own - highest) * (SCALE * LOG2E))
        total = ratio * total_ref[t] + jnp.sum(fold_rows(p, jnp.sum), axis=0, keepdims=True)
        inverse = 1.0 / total
        rim_out = [dot(rim_t[HEAD_DIM:], p_low[:, part]) for rim_t, part in zip(rims_t, parts)]
        out_t = out_ref[t] * ratio + beside(rim_out)
        attended = (out_t * inverse).astype(BF16)
        attended_ref[t] = attended
        cot_t = qc_t[HEAD_DIM:].astype(F32) * inverse
        own_cot = (cot_t * ratio).astype(BF16)
        cot_ref[t] = own_cot
        spread_ref[t] = jnp.sum(own_cot.astype(F32) * attended.astype(F32), axis=0, keepdims=True)
        cot_t = cot_t.astype(BF16)
        spread = jnp.sum(cot_t.astype(F32) * attended.astype(F32), axis=0, keepdims=True)
        cots = jnp.concatenate([zeros, cot_t], axis=0)
        product = beside([dot(rim, cots[:, part]) for rim, part in zip(rims, parts)])
        slopes = (p * (product - spread)).astype(BF16)
        query_ref[t] = beside(
            [dot(rim_t[:HEAD_DIM], slopes[:, part]) for rim_t, part in zip(rims_t, parts)]
        )
        for a, part in enumerate(parts):
            left = beside([p_low[:, part], slopes[:, part]])
            right = beside([cots[:, part], queries[:, part]])
            grad = dot(left, right, NT) * lane_scale()
            low_grad_ref[first + a] = grad[:cells].astype(BF16)
            high_grad_ref[first + a] = grad[cells:].astype(BF16)
        return carry

    lax.fori_loop(0, chunks, chunk, 0)


def backward_kernel(
    x_ref, kv_t_ref, weights_ref, attended_ref, cot_ref, spread_ref, query_ref,
    out_ref, grad_ref, slopes_scr,
):
    sectors, both, _ = x_ref.shape
    cells = both // 2
    chunks, keys, wide = weights_ref.shape
    grad_ref[...] = jnp.zeros_like(grad_ref)

    def chunk(t, carry):
        here = pl.ds(t * (wide // cells), wide // cells)
        queries_t = x_ref[here, cells:].reshape(wide, PAIR).T[:HEAD_DIM]
        zeros = jnp.zeros((HEAD_DIM, wide), BF16)
        queries = jnp.concatenate([queries_t, zeros], axis=0)
        cots = jnp.concatenate([zeros, cot_ref[t]], axis=0)
        spread = spread_ref[t]
        for block in range(0, sectors, 2):
            rows = slice(block * cells, (block + 2) * cells)
            product = dot(x_ref[block : block + 2, :cells].reshape(2 * cells, PAIR), cots)
            slopes = weights_ref[t, rows, :].astype(F32) * (product - spread)
            slopes_scr[rows, :] = slopes.astype(BF16)
        query_t = query_ref[t] + dot(kv_t_ref[:HEAD_DIM, :], slopes_scr[...])
        left = jnp.concatenate([weights_ref[t], slopes_scr[...]], axis=1)
        grad = dot(left, jnp.concatenate([cots, queries], axis=1), NT)
        grad_ref[...] += grad.reshape(sectors, cells, PAIR)
        packed = jnp.concatenate([(query_t * SCALE).astype(BF16), attended_ref[t]], axis=0)
        out_ref[here] = packed.T.reshape(wide // cells, cells, PAIR)
        return carry

    lax.fori_loop(0, chunks, chunk, 0)
    grad_ref[...] = grad_ref[...] * lane_scale().reshape(1, 1, PAIR)


def merge_kernel(out_ref, grad_ref, from_low_ref, from_high_ref, merged_ref):
    cells = out_ref.shape[1]
    merged_ref[:, :cells] = out_ref[...]
    grad = grad_ref[...] + from_low_ref[...].astype(F32) + from_high_ref[...].astype(F32)
    merged_ref[:, cells:] = grad.astype(BF16)


def unpack_kernel(merged_ref, attended_ref, query_ref, key_ref, value_ref):
    cells = attended_ref.shape[0]
    for head in range(0, HEADS, 2):
        lanes = slice(head * HEAD_DIM, (head + 2) * HEAD_DIM)
        for rows, first_ref, second_ref in (
            (slice(0, cells), query_ref, attended_ref),
            (slice(cells, 2 * cells), key_ref, value_ref),
        ):
            one, two = merged_ref[head, rows], merged_ref[head + 1, rows]
            first_ref[:, lanes] = jnp.concatenate([one[:, :HEAD_DIM], two[:, :HEAD_DIM]], axis=1)
            second_ref[:, lanes] = jnp.concatenate([one[:, HEAD_DIM:], two[:, HEAD_DIM:]], axis=1)


def cost(flops, nbytes):
    return pl.CostEstimate(flops=flops, bytes_accessed=nbytes, transcendentals=0)


def per_device(queries, key_vectors, value_vectors, cotangent, neighbour_lists, list_counts):
    _, band_rows, cycle_cols, features = queries.shape
    cells = band_rows * cycle_cols
    sectors = lax.axis_size("lon")
    bands = lax.axis_size("lat")
    chunks = sectors // CHUNK
    wide = CHUNK * cells
    keys = sectors * cells
    flat = (cells, features)
    params = pltpu.CompilerParams(vmem_limit_bytes=32 * 1024 * 1024)
    small = pltpu.CompilerParams(vmem_limit_bytes=16 * 1024 * 1024)
    struct = jax.ShapeDtypeStruct
    paired = struct((sectors, cells, PAIR), BF16)

    packed, bias = pl.pallas_call(
        pack_kernel,
        out_shape=(struct((HEADS, 2 * cells, PAIR), BF16), struct((sectors + 2, keys), F32)),
        in_specs=[SMEM] * 2 + [VMEM] * 4, out_specs=(VMEM,) * 2,
        cost_estimate=cost(0, 2 << 20), name="pack",
    )(
        neighbour_lists, list_counts, key_vectors.reshape(flat), value_vectors.reshape(flat),
        queries.reshape(flat), cotangent.reshape(flat),
    )
    x = lax.all_to_all(packed, "lon", 0, 0, tiled=True)
    kv = x[:, :cells]
    up = [(band, (band + 1) % bands) for band in range(bands)]
    down = [(target, source) for source, target in up]
    low = lax.ppermute(kv, "lat", up)
    high = lax.ppermute(kv, "lat", down)

    row_shape = struct((chunks, 1, wide), F32)
    tall_shape = struct((chunks, HEAD_DIM, wide), F32)
    tall_low = struct((chunks, HEAD_DIM, wide), BF16)

    weights, highest, total, out_t, kv_t = pl.pallas_call(
        forward_kernel,
        out_shape=(
            struct((chunks, keys, wide), BF16), row_shape, row_shape, tall_shape,
            struct((PAIR, keys), BF16),
        ),
        in_specs=[VMEM] * 2, out_specs=(VMEM,) * 5,
        scratch_shapes=[pltpu.VMEM((keys, wide), F32)],
        compiler_params=params, cost_estimate=cost(10**10, 10 << 20), name="forward",
    )(x, bias)
    attended, cot, spread, query_t, low_grad, high_grad = pl.pallas_call(
        rims_kernel,
        out_shape=(tall_low, tall_low, row_shape, tall_shape, paired, paired),
        in_specs=[VMEM] * 7, out_specs=(VMEM,) * 6,
        compiler_params=params, cost_estimate=cost(4 * 10**9, 4 << 20), name="rims",
    )(x, bias, low, high, highest, total, out_t)
    from_high = lax.ppermute(low_grad, "lat", down)
    from_low = lax.ppermute(high_grad, "lat", up)
    out, grad = pl.pallas_call(
        backward_kernel,
        out_shape=(paired, struct(paired.shape, F32)),
        in_specs=[VMEM] * 7, out_specs=(VMEM,) * 2,
        scratch_shapes=[pltpu.VMEM((keys, wide), BF16)],
        compiler_params=params, cost_estimate=cost(15 * 10**9, 12 << 20), name="backward",
    )(x, kv_t, weights, attended, cot, spread, query_t)
    merged = pl.pallas_call(
        merge_kernel, out_shape=struct((sectors, 2 * cells, PAIR), BF16),
        in_specs=[VMEM] * 4, out_specs=VMEM, compiler_params=small, cost_estimate=cost(0, 4 << 20), name="merge",
    )(out, grad, from_low, from_high)
    merged = lax.all_to_all(merged, "lon", 0, 0, tiled=True)
    results = pl.pallas_call(
        unpack_kernel, out_shape=(struct(flat, BF16),) * 4, in_specs=[VMEM], out_specs=(VMEM,) * 4,
        compiler_params=small, cost_estimate=cost(0, 2 << 20), name="unpack",
    )(merged)
    return tuple(result.reshape(queries.shape) for result in results)


def solution(mesh):
    blocks = P(None, "lat", "lon", None)
    return jax.shard_map(
        per_device, mesh=mesh, in_specs=(blocks,) * 4 + (P(), P()), out_specs=(blocks,) * 4,
        check_vma=False,
    )
```

```python
import functools

import jax
import jax.numpy as jnp
from jax import lax
from jax.experimental import pallas as pl
from jax.experimental.pallas import tpu as pltpu
from jax.sharding import PartitionSpec as P

HEADS = 16
HEAD_DIM = 64
PAIR = 2 * HEAD_DIM
SCALE = HEAD_DIM ** (-0.5)
LOG2E = 1.4426950408889634
MASKED = -1e30
CHUNK = 4
BF16 = jnp.bfloat16
F32 = jnp.float32
NN = (((1,), (0,)), ((), ()))
NT = (((1,), (1,)), ((), ()))
VMEM = pl.BlockSpec(memory_space=pltpu.VMEM)
SMEM = pl.BlockSpec(memory_space=pltpu.SMEM)


def dot(a, b, dims=NN):
    return lax.dot_general(a, b, dims, preferred_element_type=F32)


def pack_pairs(first_ref, second_ref, out_ref, rows):
    for head in range(HEADS):
        lanes = slice(head * HEAD_DIM, (head + 1) * HEAD_DIM)
        out_ref[head, rows] = jnp.concatenate([first_ref[:, lanes], second_ref[:, lanes]], axis=1)


def pack_kernel(
    lists_ref, counts_ref, key_ref, value_ref, query_ref, cot_ref, packed_ref, bias_ref
):
    cells = key_ref.shape[0]
    pack_pairs(key_ref, value_ref, packed_ref, slice(0, cells))
    pack_pairs(query_ref, cot_ref, packed_ref, slice(cells, 2 * cells))
    band = lax.axis_index("lat")
    bands, slots = lists_ref.shape
    sectors = bias_ref.shape[0] - 2
    shape = (sectors, bias_ref.shape[1])
    key_sector = lax.broadcasted_iota(jnp.int32, shape, 0)
    query_sector = lax.broadcasted_iota(jnp.int32, shape, 1) // cells
    offset = key_sector - query_sector
    offset = jnp.where(offset < 0, offset + sectors, offset)
    count = counts_ref[band]
    bias = jnp.full(shape, MASKED, F32)
    for slot in range(slots):
        named = jnp.where(slot < count, lists_ref[band, slot], -1)
        bias = jnp.where(offset == named, 0.0, bias)
    bias_ref[:sectors] = bias
    outer = jnp.where((band > 0) & (band < bands - 1), 0.0, MASKED).astype(F32)
    row = lax.broadcasted_iota(jnp.int32, (2, shape[1]), 0)
    bias_ref[sectors:] = jnp.where(row == 0, 0.0, outer)


def lane_scale():
    lane = lax.broadcasted_iota(jnp.int32, (1, PAIR), 1)
    return jnp.where(lane < HEAD_DIM, SCALE, 1.0).astype(F32)


def fold_rows(values, combine):
    return combine(values.reshape(values.shape[0] // 8, 8, values.shape[1]), axis=0)


def forward_part(start, x_ref, bias_ref, kv_t_ref, weights_ref, highest_ref, total_ref, out_ref, scores):
    sectors, both, _ = x_ref.shape
    cells = both // 2
    chunks, keys, wide = weights_ref.shape
    count = wide // cells
    blocks = [slice(block * cells, (block + 2) * cells) for block in range(0, sectors, 2)]

    def score(t, queries, rows, highest):
        block = rows.start // cells
        lanes = slice((start + t) * wide, (start + t + 1) * wide)
        s = dot(x_ref[block : block + 2, :cells].reshape(2 * cells, PAIR), queries, NT)
        s = s.reshape(2, cells, wide) + bias_ref[block : block + 2, lanes].reshape(2, 1, wide)
        s = s.reshape(2 * cells, wide)
        scores[t, rows, :] = s
        return jnp.maximum(highest, fold_rows(s, jnp.max))

    lane = lax.broadcasted_iota(jnp.int32, (1, PAIR), 1)
    highest = total = None
    for t in range(chunks + 1):
        before, before_highest = t - 1, highest
        if t < chunks:
            qc = x_ref[(start + t) * count : (start + t + 1) * count, cells:].reshape(wide, PAIR)
            queries = jnp.where(lane < HEAD_DIM, qc, jnp.zeros_like(qc))
            highest = jnp.full((8, wide), -jnp.inf, F32)
        total = jnp.zeros((8, wide), F32)
        for rows in blocks:
            if t < chunks:
                highest = score(t, queries, rows, highest)
            if t > 0:
                p = jnp.exp2((scores[before, rows, :] - before_highest) * (SCALE * LOG2E))
                total = total + fold_rows(p, jnp.sum)
                weights_ref[before, rows, :] = p.astype(BF16)
        if t > 0:
            highest_ref[before] = before_highest
            total_ref[before] = jnp.sum(total, axis=0, keepdims=True)
            out_ref[before] = dot(kv_t_ref[HEAD_DIM:, :], weights_ref[before])
        highest = jnp.max(highest, axis=0, keepdims=True)


def first_forward_kernel(x_ref, bias_ref, *refs):
    *outs, kv_t_ref, kv_ref, scores = refs
    cells = kv_ref.shape[1]
    kv_ref[...] = x_ref[kv_ref.shape[0] :, :cells]
    kv_t_ref[...] = x_ref[:, :cells].reshape(kv_t_ref.shape[1], PAIR).T
    forward_part(0, x_ref, bias_ref, kv_t_ref, *outs, scores)


def rims_kernel(
    start, x_ref, bias_ref, near_ref, far_ref, highest_ref, total_ref, out_ref, _,
    attended_ref, cot_ref, spread_ref, query_ref, near_grad_ref, far_grad_ref,
):
    sectors, both, _ = x_ref.shape
    cells = both // 2
    chunks, _, wide = out_ref.shape
    count = wide // cells
    parts = [slice(a * cells, (a + 1) * cells) for a in range(count)]

    def chunk(t, carry):
        lanes = pl.ds(pl.multiple_of((start + t) * wide, wide), wide)
        first = t * count
        qc_t = x_ref[pl.ds(start * count + first, count), cells:].reshape(wide, PAIR).T
        zeros = jnp.zeros((HEAD_DIM, wide), BF16)
        queries = jnp.concatenate([qc_t[:HEAD_DIM], zeros], axis=0)
        rims = [
            jnp.concatenate([near_ref[first + a], far_ref[first + a]], axis=0)
            for a in range(count)
        ]
        rims_t = [rim.T for rim in rims]

        def beside(values):
            return jnp.concatenate(values, axis=1)

        s = beside([dot(rim, queries[:, part]) for rim, part in zip(rims, parts)])
        s = s.reshape(2, cells, wide) + bias_ref[sectors : sectors + 2, lanes].reshape(2, 1, wide)
        s = s.reshape(2 * cells, wide)
        own = highest_ref[t]
        highest = jnp.maximum(own, jnp.max(fold_rows(s, jnp.max), axis=0, keepdims=True))
        p = jnp.exp2((s - highest) * (SCALE * LOG2E))
        p_low = p.astype(BF16)
        ratio = jnp.exp2((own - highest) * (SCALE * LOG2E))
        total = ratio * total_ref[t] + jnp.sum(fold_rows(p, jnp.sum), axis=0, keepdims=True)
        inverse = 1.0 / total
        rim_out = [dot(rim_t[HEAD_DIM:], p_low[:, part]) for rim_t, part in zip(rims_t, parts)]
        out_t = out_ref[t] * ratio + beside(rim_out)
        attended = (out_t * inverse).astype(BF16)
        attended_ref[t] = attended
        cot_t = qc_t[HEAD_DIM:].astype(F32) * inverse
        own_cot = (cot_t * ratio).astype(BF16)
        cot_ref[t] = own_cot
        spread_ref[t] = jnp.sum(own_cot.astype(F32) * attended.astype(F32), axis=0, keepdims=True)
        cot_t = cot_t.astype(BF16)
        spread = jnp.sum(cot_t.astype(F32) * attended.astype(F32), axis=0, keepdims=True)
        cots = jnp.concatenate([zeros, cot_t], axis=0)
        product = beside([dot(rim, cots[:, part]) for rim, part in zip(rims, parts)])
        slopes = (p * (product - spread)).astype(BF16)
        query_ref[t] = beside(
            [dot(rim_t[:HEAD_DIM], slopes[:, part]) for rim_t, part in zip(rims_t, parts)]
        )
        for a, part in enumerate(parts):
            left = beside([p_low[:, part], slopes[:, part]])
            right = beside([cots[:, part], queries[:, part]])
            grad = dot(left, right, NT) * lane_scale()
            near_grad_ref[first + a] = grad[:cells].astype(BF16)
            far_grad_ref[first + a] = grad[cells:].astype(BF16)
        return carry

    lax.fori_loop(0, chunks, chunk, 0)


def backward_kernel(
    start, x_ref, kv_t_ref, weights_ref, attended_ref, cot_ref, spread_ref, query_ref, *refs
):
    *before, out_ref, grad_ref, slopes_scr = refs
    sectors, both, _ = x_ref.shape
    cells = both // 2
    chunks, keys, wide = weights_ref.shape
    grad_ref[...] = before[0][...] if before else jnp.zeros_like(grad_ref)

    def chunk(t, carry):
        count = wide // cells
        queries_t = x_ref[pl.ds((start + t) * count, count), cells:].reshape(wide, PAIR).T[:HEAD_DIM]
        zeros = jnp.zeros((HEAD_DIM, wide), BF16)
        queries = jnp.concatenate([queries_t, zeros], axis=0)
        cots = jnp.concatenate([zeros, cot_ref[t]], axis=0)
        spread = spread_ref[t]
        for block in range(0, sectors, 2):
            rows = slice(block * cells, (block + 2) * cells)
            product = dot(x_ref[block : block + 2, :cells].reshape(2 * cells, PAIR), cots)
            slopes = weights_ref[t, rows, :].astype(F32) * (product - spread)
            slopes_scr[rows, :] = slopes.astype(BF16)
        query_t = query_ref[t] + dot(kv_t_ref[:HEAD_DIM, :], slopes_scr[...])
        left = jnp.concatenate([weights_ref[t], slopes_scr[...]], axis=1)
        grad = dot(left, jnp.concatenate([cots, queries], axis=1), NT)
        grad_ref[...] += grad.reshape(sectors, cells, PAIR)
        packed = jnp.concatenate([(query_t * SCALE).astype(BF16), attended_ref[t]], axis=0)
        out_ref[pl.ds(t * count, count)] = packed.T.reshape(count, cells, PAIR)
        return carry

    lax.fori_loop(0, chunks, chunk, 0)


def merge_kernel(grad_ref, *refs):
    *part_refs, merged_ref = refs
    cells = grad_ref.shape[1]
    start = 0
    for out_ref, near_ref, far_ref in zip(part_refs[::3], part_refs[1::3], part_refs[2::3]):
        part = slice(start, start + out_ref.shape[0])
        merged_ref[part, :cells] = out_ref[...]
        grad = grad_ref[part] * lane_scale().reshape(1, 1, PAIR)
        grad = grad + near_ref[...].astype(F32) + far_ref[...].astype(F32)
        merged_ref[part, cells:] = grad.astype(BF16)
        start = part.stop


def unpack_kernel(merged_ref, attended_ref, query_ref, key_ref, value_ref):
    cells = attended_ref.shape[0]
    for head in range(0, HEADS, 2):
        lanes = slice(head * HEAD_DIM, (head + 2) * HEAD_DIM)
        for rows, first_ref, second_ref in (
            (slice(0, cells), query_ref, attended_ref),
            (slice(cells, 2 * cells), key_ref, value_ref),
        ):
            one, two = merged_ref[head, rows], merged_ref[head + 1, rows]
            first_ref[:, lanes] = jnp.concatenate([one[:, :HEAD_DIM], two[:, :HEAD_DIM]], axis=1)
            second_ref[:, lanes] = jnp.concatenate([one[:, HEAD_DIM:], two[:, HEAD_DIM:]], axis=1)


def cost(flops, nbytes):
    return pl.CostEstimate(flops=flops, bytes_accessed=nbytes, transcendentals=0)


def per_device(queries, key_vectors, value_vectors, cotangent, neighbour_lists, list_counts):
    _, band_rows, cycle_cols, features = queries.shape
    cells = band_rows * cycle_cols
    sectors = lax.axis_size("lon")
    bands = lax.axis_size("lat")
    part = sectors // 2
    steps = part // CHUNK
    wide = CHUNK * cells
    keys = sectors * cells
    flat = (cells, features)
    params = pltpu.CompilerParams(vmem_limit_bytes=24 * 1024 * 1024)
    struct = jax.ShapeDtypeStruct

    def both_ways(to_near, to_far):
        return lax.ppermute(to_near, "lat", near), lax.ppermute(to_far, "lat", far)

    def call(kernel, outs, args, name, flops, specs=None, scratch=(), compiler_params=params):
        return pl.pallas_call(
            kernel, out_shape=outs, in_specs=specs or [VMEM] * len(args),
            out_specs=(VMEM,) * len(outs), scratch_shapes=scratch,
            compiler_params=compiler_params, cost_estimate=cost(flops, 4 << 20), name=name,
        )(*args)

    packed, bias = call(
        pack_kernel,
        (struct((HEADS, 2 * cells, PAIR), BF16), struct((sectors + 2, keys), F32)),
        (neighbour_lists, list_counts)
        + tuple(a.reshape(flat) for a in (key_vectors, value_vectors, queries, cotangent)),
        "pack", 0, [SMEM] * 2 + [VMEM] * 4, compiler_params=None,
    )
    x = lax.all_to_all(packed, "lon", 0, 0, tiled=True)
    near = [(band, band ^ 1) for band in range(bands)]
    far = [(band, ((band + 1) ^ 1) - 1) for band in range(1, bands - 1)]
    far += [(0, bands - 1), (bands - 1, 0)]

    row = struct((steps, 1, wide), F32)
    tall = struct((steps, HEAD_DIM, wide), F32)
    tall_low = struct(tall.shape, BF16)
    by_part = struct((part, cells, PAIR), BF16)
    ahead = (struct((steps, keys, wide), BF16), row, row, tall)
    scores = [pltpu.VMEM((steps, keys, wide), F32)]

    kv = x[:part, :cells]
    rims = [both_ways(kv, kv)]
    weights, *stats, kv_t, kv = call(
        first_forward_kernel, ahead + (struct((PAIR, keys), BF16), by_part), (x, bias),
        "forward", 5 * 10**9, scratch=scores,
    )
    forward = [(weights, stats)]
    rims.append(both_ways(kv, kv))
    weights, *stats = call(
        functools.partial(forward_part, steps), ahead, (x, bias, kv_t), "forward", 5 * 10**9,
        scratch=scores,
    )
    forward.append((weights, stats))
    last = stats[0]
    before, returned = (), []
    for i, (weights, stats) in enumerate(forward):
        *for_queries, near_grad, far_grad = call(
            functools.partial(rims_kernel, i * steps),
            (tall_low, tall_low, row, tall, by_part, by_part),
            (x, bias) + rims[i] + tuple(stats) + (last,), "rims", 10**9,
        )
        from_rims = both_ways(near_grad, far_grad)
        out, grad = call(
            functools.partial(backward_kernel, i * steps),
            (by_part, struct((sectors, cells, PAIR), F32)),
            (x, kv_t, weights) + tuple(for_queries) + before, "backward", 5 * 10**9,
            scratch=[pltpu.VMEM((keys, wide), BF16)],
        )
        before, last = (grad,) + from_rims, out
        returned += [out, *from_rims]
    (merged,) = call(
        merge_kernel, (struct((sectors, 2 * cells, PAIR), BF16),), (grad, *returned), "merge", 0
    )
    merged = lax.all_to_all(merged, "lon", 0, 0, tiled=True)
    results = call(unpack_kernel, (struct(flat, BF16),) * 4, (merged,), "unpack", 0)
    return tuple(result.reshape(queries.shape) for result in results)


def solution(mesh):
    blocks = P(None, "lat", "lon", None)
    return jax.shard_map(
        per_device, mesh=mesh, in_specs=(blocks,) * 4 + (P(), P()), out_specs=(blocks,) * 4,
        check_vma=False,
    )
```

```python
import functools

import jax
import jax.numpy as jnp
from jax import lax
from jax.experimental import pallas as pl
from jax.experimental.pallas import tpu as pltpu
from jax.sharding import PartitionSpec as P

HEADS = 16
HEAD_DIM = 64
PAIR = 2 * HEAD_DIM
SCALE = HEAD_DIM ** (-0.5)
LOG2E = 1.4426950408889634
MASKED = -1e30
CHUNK = 4
BF16 = jnp.bfloat16
F32 = jnp.float32
NN = (((1,), (0,)), ((), ()))
NT = (((1,), (1,)), ((), ()))
VMEM = pl.BlockSpec(memory_space=pltpu.VMEM)
SMEM = pl.BlockSpec(memory_space=pltpu.SMEM)
ANY = pl.BlockSpec(memory_space=pl.ANY)


def dot(a, b, dims=NN):
    return lax.dot_general(a, b, dims, preferred_element_type=F32)


def pack_pairs(first_ref, second_ref, out_ref):
    for head in range(HEADS):
        lanes = slice(head * HEAD_DIM, (head + 1) * HEAD_DIM)
        out_ref[head] = jnp.concatenate([first_ref[:, lanes], second_ref[:, lanes]], axis=1)


def pack_kernel(key_ref, value_ref, query_ref, cot_ref, packed_ref, held, pairs, in_sems, out_sems):
    cells = key_ref.shape[0]
    arrivals = [
        pltpu.make_async_copy(ref, held.at[i], in_sems.at[i])
        for i, ref in enumerate((key_ref, value_ref, query_ref, cot_ref))
    ]
    for arrival in arrivals:
        arrival.start()
    departures = []
    for i in range(2):
        arrivals[2 * i].wait()
        arrivals[2 * i + 1].wait()
        rows = pl.ds(i * cells, cells)
        pack_pairs(held.at[2 * i], held.at[2 * i + 1], pairs.at[i])
        departures.append(
            pltpu.make_async_copy(pairs.at[i], packed_ref.at[:, rows], out_sems.at[i])
        )
        departures[i].start()
    for departure in departures:
        departure.wait()


def bias_kernel(lists_ref, counts_ref, bias_ref):
    band = lax.axis_index("lat")
    bands, slots = lists_ref.shape
    sectors = bias_ref.shape[0] - 2
    shape = (sectors, bias_ref.shape[1])
    cells = shape[1] // sectors
    key_sector = lax.broadcasted_iota(jnp.int32, shape, 0)
    query_sector = lax.broadcasted_iota(jnp.int32, shape, 1) // cells
    offset = key_sector - query_sector
    offset = jnp.where(offset < 0, offset + sectors, offset)
    count = counts_ref[band]
    bias = jnp.full(shape, MASKED, F32)
    for slot in range(slots):
        named = jnp.where(slot < count, lists_ref[band, slot], -1)
        bias = jnp.where(offset == named, 0.0, bias)
    bias_ref[:sectors] = bias
    outer = jnp.where((band > 0) & (band < bands - 1), 0.0, MASKED).astype(F32)
    row = lax.broadcasted_iota(jnp.int32, (2, shape[1]), 0)
    bias_ref[sectors:] = jnp.where(row == 0, 0.0, outer)


def lane_scale():
    lane = lax.broadcasted_iota(jnp.int32, (1, PAIR), 1)
    return jnp.where(lane < HEAD_DIM, SCALE, 1.0).astype(F32)


def fold_rows(values, combine):
    return combine(values.reshape(values.shape[0] // 8, 8, values.shape[1]), axis=0)


def forward_part(start, x_ref, bias_ref, kv_t_ref, weights_ref, highest_ref, total_ref, out_ref, scores):
    sectors, both, _ = x_ref.shape
    cells = both // 2
    chunks, keys, wide = weights_ref.shape
    count = wide // cells
    blocks = [slice(block * cells, (block + 2) * cells) for block in range(0, sectors, 2)]

    def score(t, queries, rows, highest):
        block = rows.start // cells
        lanes = slice((start + t) * wide, (start + t + 1) * wide)
        s = dot(x_ref[block : block + 2, :cells].reshape(2 * cells, PAIR), queries, NT)
        s = s.reshape(2, cells, wide) + bias_ref[block : block + 2, lanes].reshape(2, 1, wide)
        s = s.reshape(2 * cells, wide)
        scores[t, rows, :] = s
        return jnp.maximum(highest, fold_rows(s, jnp.max))

    lane = lax.broadcasted_iota(jnp.int32, (1, PAIR), 1)
    highest = total = None
    for t in range(chunks + 1):
        before, before_highest = t - 1, highest
        if t < chunks:
            qc = x_ref[(start + t) * count : (start + t + 1) * count, cells:].reshape(wide, PAIR)
            queries = jnp.where(lane < HEAD_DIM, qc, jnp.zeros_like(qc))
            highest = jnp.full((8, wide), -jnp.inf, F32)
        total = jnp.zeros((8, wide), F32)
        for rows in blocks:
            if t < chunks:
                highest = score(t, queries, rows, highest)
            if t > 0:
                p = jnp.exp2((scores[before, rows, :] - before_highest) * (SCALE * LOG2E))
                total = total + fold_rows(p, jnp.sum)
                weights_ref[before, rows, :] = p.astype(BF16)
        if t > 0:
            highest_ref[before] = before_highest
            total_ref[before] = jnp.sum(total, axis=0, keepdims=True)
            out_ref[before] = dot(kv_t_ref[HEAD_DIM:, :], weights_ref[before])
        highest = jnp.max(highest, axis=0, keepdims=True)


def first_forward_kernel(x_ref, bias_ref, *refs):
    *outs, kv_t_ref, kv_ref, scores = refs
    cells = kv_ref.shape[1]
    kv_ref[...] = x_ref[kv_ref.shape[0] :, :cells]
    kv_t_ref[...] = x_ref[:, :cells].reshape(kv_t_ref.shape[1], PAIR).T
    forward_part(0, x_ref, bias_ref, kv_t_ref, *outs, scores)


def rims_kernel(
    start, x_ref, bias_ref, near_ref, far_ref, highest_ref, total_ref, out_ref, _,
    attended_ref, cot_ref, spread_ref, query_ref, near_grad_ref, far_grad_ref,
):
    sectors, both, _ = x_ref.shape
    cells = both // 2
    chunks, _, wide = out_ref.shape
    count = wide // cells
    parts = [slice(a * cells, (a + 1) * cells) for a in range(count)]

    def chunk(t, carry):
        lanes = pl.ds(pl.multiple_of((start + t) * wide, wide), wide)
        first = t * count
        qc_t = x_ref[pl.ds(start * count + first, count), cells:].reshape(wide, PAIR).T
        zeros = jnp.zeros((HEAD_DIM, wide), BF16)
        queries = jnp.concatenate([qc_t[:HEAD_DIM], zeros], axis=0)
        rims = [
            jnp.concatenate([near_ref[first + a], far_ref[first + a]], axis=0)
            for a in range(count)
        ]
        rims_t = [rim.T for rim in rims]

        def beside(values):
            return jnp.concatenate(values, axis=1)

        s = beside([dot(rim, queries[:, part]) for rim, part in zip(rims, parts)])
        s = s.reshape(2, cells, wide) + bias_ref[sectors : sectors + 2, lanes].reshape(2, 1, wide)
        s = s.reshape(2 * cells, wide)
        own = highest_ref[t]
        highest = jnp.maximum(own, jnp.max(fold_rows(s, jnp.max), axis=0, keepdims=True))
        p = jnp.exp2((s - highest) * (SCALE * LOG2E))
        p_low = p.astype(BF16)
        ratio = jnp.exp2((own - highest) * (SCALE * LOG2E))
        total = ratio * total_ref[t] + jnp.sum(fold_rows(p, jnp.sum), axis=0, keepdims=True)
        inverse = 1.0 / total
        rim_out = [dot(rim_t[HEAD_DIM:], p_low[:, part]) for rim_t, part in zip(rims_t, parts)]
        out_t = out_ref[t] * ratio + beside(rim_out)
        attended = (out_t * inverse).astype(BF16)
        attended_ref[t] = attended
        cot_t = qc_t[HEAD_DIM:].astype(F32) * inverse
        own_cot = (cot_t * ratio).astype(BF16)
        cot_ref[t] = own_cot
        spread_ref[t] = jnp.sum(own_cot.astype(F32) * attended.astype(F32), axis=0, keepdims=True)
        cot_t = cot_t.astype(BF16)
        spread = jnp.sum(cot_t.astype(F32) * attended.astype(F32), axis=0, keepdims=True)
        cots = jnp.concatenate([zeros, cot_t], axis=0)
        product = beside([dot(rim, cots[:, part]) for rim, part in zip(rims, parts)])
        slopes = (p * (product - spread)).astype(BF16)
        query_ref[t] = beside(
            [dot(rim_t[:HEAD_DIM], slopes[:, part]) for rim_t, part in zip(rims_t, parts)]
        )
        for a, part in enumerate(parts):
            left = beside([p_low[:, part], slopes[:, part]])
            right = beside([cots[:, part], queries[:, part]])
            grad = dot(left, right, NT) * lane_scale()
            near_grad_ref[first + a] = grad[:cells].astype(BF16)
            far_grad_ref[first + a] = grad[cells:].astype(BF16)
        return carry

    lax.fori_loop(0, chunks, chunk, 0, unroll=True)


def backward_kernel(
    start, x_ref, kv_t_ref, weights_ref, attended_ref, cot_ref, spread_ref, query_ref, *refs
):
    *before, out_ref, grad_ref, slopes_scr = refs
    sectors, both, _ = x_ref.shape
    cells = both // 2
    chunks, keys, wide = weights_ref.shape
    grad_ref[...] = before[0][...] if before else jnp.zeros_like(grad_ref)

    def chunk(t, carry):
        count = wide // cells
        queries_t = x_ref[pl.ds((start + t) * count, count), cells:].reshape(wide, PAIR).T[:HEAD_DIM]
        zeros = jnp.zeros((HEAD_DIM, wide), BF16)
        queries = jnp.concatenate([queries_t, zeros], axis=0)
        cots = jnp.concatenate([zeros, cot_ref[t]], axis=0)
        spread = spread_ref[t]
        for block in range(0, sectors, 2):
            rows = slice(block * cells, (block + 2) * cells)
            product = dot(x_ref[block : block + 2, :cells].reshape(2 * cells, PAIR), cots)
            slopes = weights_ref[t, rows, :].astype(F32) * (product - spread)
            slopes_scr[rows, :] = slopes.astype(BF16)
        query_t = query_ref[t] + dot(kv_t_ref[:HEAD_DIM, :], slopes_scr[...])
        left = jnp.concatenate([weights_ref[t], slopes_scr[...]], axis=1)
        grad = dot(left, jnp.concatenate([cots, queries], axis=1), NT)
        grad_ref[...] += grad.reshape(sectors, cells, PAIR)
        packed = jnp.concatenate([(query_t * SCALE).astype(BF16), attended_ref[t]], axis=0)
        out_ref[pl.ds(t * count, count)] = packed.T.reshape(count, cells, PAIR)
        return carry

    lax.fori_loop(0, chunks, chunk, 0, unroll=True)


def merge_kernel(grad_ref, *refs):
    *part_refs, merged_ref = refs
    cells = grad_ref.shape[1]
    start = 0
    for out_ref, near_ref, far_ref in zip(part_refs[::3], part_refs[1::3], part_refs[2::3]):
        part = slice(start, start + out_ref.shape[0])
        merged_ref[part, :cells] = out_ref[...]
        grad = grad_ref[part] * lane_scale().reshape(1, 1, PAIR)
        grad = grad + near_ref[...].astype(F32) + far_ref[...].astype(F32)
        merged_ref[part, cells:] = grad.astype(BF16)
        start = part.stop


def unpack_kernel(merged_ref, attended_ref, query_ref, key_ref, value_ref):
    cells = attended_ref.shape[0]
    for head in range(0, HEADS, 2):
        lanes = slice(head * HEAD_DIM, (head + 2) * HEAD_DIM)
        for rows, first_ref, second_ref in (
            (slice(0, cells), query_ref, attended_ref),
            (slice(cells, 2 * cells), key_ref, value_ref),
        ):
            one, two = merged_ref[head, rows], merged_ref[head + 1, rows]
            first_ref[:, lanes] = jnp.concatenate([one[:, :HEAD_DIM], two[:, :HEAD_DIM]], axis=1)
            second_ref[:, lanes] = jnp.concatenate([one[:, HEAD_DIM:], two[:, HEAD_DIM:]], axis=1)


def cost(flops, nbytes):
    return pl.CostEstimate(flops=flops, bytes_accessed=nbytes, transcendentals=0)


def per_device(queries, key_vectors, value_vectors, cotangent, neighbour_lists, list_counts):
    _, band_rows, cycle_cols, features = queries.shape
    cells = band_rows * cycle_cols
    sectors = lax.axis_size("lon")
    bands = lax.axis_size("lat")
    part = sectors // 2
    steps = part // CHUNK
    wide = CHUNK * cells
    keys = sectors * cells
    flat = (cells, features)
    params = pltpu.CompilerParams(vmem_limit_bytes=24 * 1024 * 1024)
    struct = jax.ShapeDtypeStruct

    def both_ways(to_near, to_far):
        return lax.ppermute(to_near, "lat", near), lax.ppermute(to_far, "lat", far)

    def call(kernel, outs, args, name, flops, specs=None, scratch=(), compiler_params=params):
        return pl.pallas_call(
            kernel, out_shape=outs, in_specs=specs or [VMEM] * len(args),
            out_specs=(VMEM,) * len(outs), scratch_shapes=scratch,
            compiler_params=compiler_params, cost_estimate=cost(flops, 4 << 20), name=name,
        )(*args)

    packed = pl.pallas_call(
        pack_kernel, out_shape=struct((HEADS, 2 * cells, PAIR), BF16),
        in_specs=[ANY] * 4, out_specs=ANY,
        scratch_shapes=[
            pltpu.VMEM((4,) + flat, BF16), pltpu.VMEM((2, HEADS, cells, PAIR), BF16),
            pltpu.SemaphoreType.DMA((4,)), pltpu.SemaphoreType.DMA((2,)),
        ],
        cost_estimate=cost(0, 2 << 20), name="pack",
    )(*(a.reshape(flat) for a in (key_vectors, value_vectors, queries, cotangent)))
    (bias,) = call(
        bias_kernel, (struct((sectors + 2, keys), F32),), (neighbour_lists, list_counts),
        "bias", 10**8, [SMEM] * 2,
    )
    x = lax.all_to_all(packed, "lon", 0, 0, tiled=True)
    near = [(band, band ^ 1) for band in range(bands)]
    far = [(band, ((band + 1) ^ 1) - 1) for band in range(1, bands - 1)]
    far += [(0, bands - 1), (bands - 1, 0)]

    row = struct((steps, 1, wide), F32)
    tall = struct((steps, HEAD_DIM, wide), F32)
    tall_low = struct(tall.shape, BF16)
    by_part = struct((part, cells, PAIR), BF16)
    ahead = (struct((steps, keys, wide), BF16), row, row, tall)
    scores = [pltpu.VMEM((steps, keys, wide), F32)]

    kv = x[:part, :cells]
    rims = [both_ways(kv, kv)]
    weights, *stats, kv_t, kv = call(
        first_forward_kernel, ahead + (struct((PAIR, keys), BF16), by_part), (x, bias),
        "forward", 5 * 10**9, scratch=scores,
    )
    forward = [(weights, stats)]
    rims.append(both_ways(kv, kv))
    weights, *stats = call(
        functools.partial(forward_part, steps), ahead, (x, bias, kv_t), "forward", 5 * 10**9,
        scratch=scores,
    )
    forward.append((weights, stats))
    last = stats[0]
    before, returned = (), []
    for i, (weights, stats) in enumerate(forward):
        *for_queries, near_grad, far_grad = call(
            functools.partial(rims_kernel, i * steps),
            (tall_low, tall_low, row, tall, by_part, by_part),
            (x, bias) + rims[i] + tuple(stats) + (last,), "rims", 10**9,
        )
        from_rims = both_ways(near_grad, far_grad)
        out, grad = call(
            functools.partial(backward_kernel, i * steps),
            (by_part, struct((sectors, cells, PAIR), F32)),
            (x, kv_t, weights) + tuple(for_queries) + before, "backward", 5 * 10**9,
            scratch=[pltpu.VMEM((keys, wide), BF16)],
        )
        before, last = (grad,) + from_rims, out
        returned += [out, *from_rims]
    (merged,) = call(
        merge_kernel, (struct((sectors, 2 * cells, PAIR), BF16),), (grad, *returned), "merge", 0
    )
    merged = lax.all_to_all(merged, "lon", 0, 0, tiled=True)
    results = call(unpack_kernel, (struct(flat, BF16),) * 4, (merged,), "unpack", 0)
    return tuple(result.reshape(queries.shape) for result in results)


def solution(mesh):
    blocks = P(None, "lat", "lon", None)
    return jax.shard_map(
        per_device, mesh=mesh, in_specs=(blocks,) * 4 + (P(), P()), out_specs=(blocks,) * 4,
        check_vma=False,
    )
```

```python
import functools

import jax
import jax.numpy as jnp
from jax import lax
from jax.experimental import pallas as pl
from jax.experimental.pallas import tpu as pltpu
from jax.sharding import PartitionSpec as P

HEADS = 16
HEAD_DIM = 64
PAIR = 2 * HEAD_DIM
SCALE = HEAD_DIM ** (-0.5)
LOG2E = 1.4426950408889634
MASKED = -1e30
CHUNK = 4
PLANS = ((((0, 0),),), (((0, 1), (1, 0), (1, 1)),))
BF16 = jnp.bfloat16
F32 = jnp.float32
NN = (((1,), (0,)), ((), ()))
NT = (((1,), (1,)), ((), ()))
VMEM = pl.BlockSpec(memory_space=pltpu.VMEM)
SMEM = pl.BlockSpec(memory_space=pltpu.SMEM)
ANY = pl.BlockSpec(memory_space=pl.ANY)


def dot(a, b, dims=NN):
    return lax.dot_general(a, b, dims, preferred_element_type=F32)


def pack_pairs(first_ref, second_ref, out_ref):
    for head in range(HEADS):
        lanes = slice(head * HEAD_DIM, (head + 1) * HEAD_DIM)
        out_ref[head] = jnp.concatenate([first_ref[:, lanes], second_ref[:, lanes]], axis=1)


def pack_kernel(key_ref, value_ref, query_ref, cot_ref, packed_ref, held, pairs, in_sems, out_sems):
    cells = key_ref.shape[0]
    arrivals = [
        pltpu.make_async_copy(ref, held.at[i], in_sems.at[i])
        for i, ref in enumerate((key_ref, value_ref, query_ref, cot_ref))
    ]
    for arrival in arrivals:
        arrival.start()
    departures = []
    for i in range(2):
        arrivals[2 * i].wait()
        arrivals[2 * i + 1].wait()
        rows = pl.ds(i * cells, cells)
        pack_pairs(held.at[2 * i], held.at[2 * i + 1], pairs.at[i])
        departures.append(
            pltpu.make_async_copy(pairs.at[i], packed_ref.at[:, rows], out_sems.at[i])
        )
        departures[i].start()
    for departure in departures:
        departure.wait()


def bias_kernel(lists_ref, counts_ref, bias_ref):
    band = lax.axis_index("lat")
    bands, slots = lists_ref.shape
    sectors = bias_ref.shape[0] - 2
    shape = (sectors, bias_ref.shape[1])
    cells = shape[1] // sectors
    key_sector = lax.broadcasted_iota(jnp.int32, shape, 0)
    query_sector = lax.broadcasted_iota(jnp.int32, shape, 1) // cells
    offset = key_sector - query_sector
    offset = jnp.where(offset < 0, offset + sectors, offset)
    count = counts_ref[band]
    bias = jnp.full(shape, MASKED, F32)
    for slot in range(slots):
        named = jnp.where(slot < count, lists_ref[band, slot], -1)
        bias = jnp.where(offset == named, 0.0, bias)
    bias_ref[:sectors] = bias
    outer = jnp.where((band > 0) & (band < bands - 1), 0.0, MASKED).astype(F32)
    row = lax.broadcasted_iota(jnp.int32, (2, shape[1]), 0)
    bias_ref[sectors:] = jnp.where(row == 0, 0.0, outer)


def lane_scale():
    lane = lax.broadcasted_iota(jnp.int32, (1, PAIR), 1)
    return jnp.where(lane < HEAD_DIM, SCALE, 1.0).astype(F32)


def fold_rows(values, combine):
    return combine(values.reshape(values.shape[0] // 8, 8, values.shape[1]), axis=0)


def forward_part(start, x_ref, bias_ref, kv_t_ref, weights_ref, highest_ref, total_ref, out_ref, scores):
    sectors, both, _ = x_ref.shape
    cells = both // 2
    chunks, keys, wide = weights_ref.shape
    count = wide // cells
    blocks = [slice(block * cells, (block + 2) * cells) for block in range(0, sectors, 2)]

    def score(t, queries, rows, highest):
        block = rows.start // cells
        lanes = slice((start + t) * wide, (start + t + 1) * wide)
        s = dot(x_ref[block : block + 2, :cells].reshape(2 * cells, PAIR), queries, NT)
        s = s.reshape(2, cells, wide) + bias_ref[block : block + 2, lanes].reshape(2, 1, wide)
        s = s.reshape(2 * cells, wide)
        scores[t, rows, :] = s
        return jnp.maximum(highest, fold_rows(s, jnp.max))

    lane = lax.broadcasted_iota(jnp.int32, (1, PAIR), 1)
    highest = total = None
    for t in range(chunks + 1):
        before, before_highest = t - 1, highest
        if t < chunks:
            qc = x_ref[(start + t) * count : (start + t + 1) * count, cells:].reshape(wide, PAIR)
            queries = jnp.where(lane < HEAD_DIM, qc, jnp.zeros_like(qc))
            highest = jnp.full((8, wide), -jnp.inf, F32)
        total = jnp.zeros((8, wide), F32)
        for rows in blocks:
            if t < chunks:
                highest = score(t, queries, rows, highest)
            if t > 0:
                p = jnp.exp2((scores[before, rows, :] - before_highest) * (SCALE * LOG2E))
                total = total + fold_rows(p, jnp.sum)
                weights_ref[before, rows, :] = p.astype(BF16)
        if t > 0:
            highest_ref[before] = before_highest
            total_ref[before] = jnp.sum(total, axis=0, keepdims=True)
            out_ref[before] = dot(kv_t_ref[HEAD_DIM:, :], weights_ref[before])
        highest = jnp.max(highest, axis=0, keepdims=True)


def first_forward_kernel(x_ref, bias_ref, *refs):
    *outs, kv_t_ref, kv_ref, scores = refs
    cells = kv_ref.shape[1]
    kv_ref[...] = x_ref[kv_ref.shape[0] :, :cells]
    kv_t_ref[...] = x_ref[:, :cells].reshape(kv_t_ref.shape[1], PAIR).T
    forward_part(0, x_ref, bias_ref, kv_t_ref, *outs, scores)


def rims_kernel(
    start, x_ref, bias_ref, near_ref, far_ref, highest_ref, total_ref, out_ref, _,
    attended_ref, cot_ref, spread_ref, query_ref, near_grad_ref, far_grad_ref,
):
    sectors, both, _ = x_ref.shape
    cells = both // 2
    chunks, _, narrow = out_ref.shape
    wide = chunks * narrow
    count = wide // cells
    parts = [slice(a * cells, (a + 1) * cells) for a in range(count)]
    first = start * (narrow // cells)

    def beside(values):
        return jnp.concatenate(values, axis=1)

    def read(ref):
        return beside([ref[t] for t in range(chunks)])

    def write(ref, value):
        for t in range(chunks):
            ref[t] = value[:, t * narrow : (t + 1) * narrow]

    qc_t = x_ref[first : first + count, cells:].reshape(wide, PAIR).T
    zeros = jnp.zeros((HEAD_DIM, wide), BF16)
    queries = jnp.concatenate([qc_t[:HEAD_DIM], zeros], axis=0)
    rims = [jnp.concatenate([near_ref[a], far_ref[a]], axis=0) for a in range(count)]
    rims_t = [rim.T for rim in rims]
    bias = bias_ref[sectors : sectors + 2, first * cells : (first + count) * cells]
    s = beside([dot(rim, queries[:, part]) for rim, part in zip(rims, parts)])
    s = (s.reshape(2, cells, wide) + bias.reshape(2, 1, wide)).reshape(2 * cells, wide)
    own = read(highest_ref)
    highest = jnp.maximum(own, jnp.max(fold_rows(s, jnp.max), axis=0, keepdims=True))
    p = jnp.exp2((s - highest) * (SCALE * LOG2E))
    p_low = p.astype(BF16)
    ratio = jnp.exp2((own - highest) * (SCALE * LOG2E))
    total = ratio * read(total_ref) + jnp.sum(fold_rows(p, jnp.sum), axis=0, keepdims=True)
    inverse = 1.0 / total
    rim_out = [dot(rim_t[HEAD_DIM:], p_low[:, part]) for rim_t, part in zip(rims_t, parts)]
    out_t = read(out_ref) * ratio + beside(rim_out)
    attended = (out_t * inverse).astype(BF16)
    write(attended_ref, attended)
    cot_t = qc_t[HEAD_DIM:].astype(F32) * inverse
    own_cot = (cot_t * ratio).astype(BF16)
    write(cot_ref, own_cot)
    own_spread = own_cot.astype(F32) * attended.astype(F32)
    write(spread_ref, jnp.sum(own_spread, axis=0, keepdims=True))
    cot_t = cot_t.astype(BF16)
    spread = jnp.sum(cot_t.astype(F32) * attended.astype(F32), axis=0, keepdims=True)
    cots = jnp.concatenate([zeros, cot_t], axis=0)
    product = beside([dot(rim, cots[:, part]) for rim, part in zip(rims, parts)])
    slopes = (p * (product - spread)).astype(BF16)
    for a, part in enumerate(parts):
        left = beside([p_low[:, part], slopes[:, part]])
        right = beside([cots[:, part], queries[:, part]])
        grad = dot(left, right, NT) * lane_scale()
        near_grad_ref[a] = grad[:cells].astype(BF16)
        far_grad_ref[a] = grad[cells:].astype(BF16)
    query_t = [dot(rim_t[:HEAD_DIM], slopes[:, part]) for rim_t, part in zip(rims_t, parts)]
    write(query_ref, beside(query_t))


def backward_kernel(plan, steps, x_ref, kv_t_ref, *refs):
    parts = 1 + max(part for part, _ in plan)
    groups = [refs[5 * i : 5 * i + 5] for i in range(parts)]
    *before, out_ref, grad_ref, slopes_scr = refs[5 * parts :]
    sectors, both, _ = x_ref.shape
    cells = both // 2
    _, keys, wide = slopes_scr.shape
    count = wide // cells
    grad_ref[...] = before[0][...] if before else jnp.zeros_like(grad_ref)
    zeros = jnp.zeros((HEAD_DIM, wide), BF16)

    def load(part, t):
        first = (part * steps + t) * count
        queries_t = x_ref[first : first + count, cells:].reshape(wide, PAIR).T[:HEAD_DIM]
        queries = jnp.concatenate([queries_t, zeros], axis=0)
        cots = jnp.concatenate([zeros, groups[part][2][t]], axis=0)
        return cots, jnp.concatenate([cots, queries], axis=1), groups[part][3][t]

    def make_slopes(i, cots, spread, block):
        part, t = plan[i]
        rows = slice(block * cells, (block + 2) * cells)
        product = dot(x_ref[block : block + 2, :cells].reshape(2 * cells, PAIR), cots)
        slopes = groups[part][0][t, rows, :].astype(F32) * (product - spread)
        slopes_scr[i % 2, rows, :] = slopes.astype(BF16)

    def add_grads(i, right, rows):
        part, t = plan[i]
        left = jnp.concatenate([groups[part][0][t, rows, :], slopes_scr[i % 2, rows, :]], axis=1)
        first, last = rows.start // cells, rows.stop // cells
        grad_ref[first:last] += dot(left, right, NT).reshape(last - first, cells, PAIR)

    def finish(i):
        part, t = plan[i]
        attended_ref, query_ref = groups[part][1], groups[part][4]
        query_t = query_ref[t] + dot(kv_t_ref[:HEAD_DIM, :], slopes_scr[i % 2])
        packed = jnp.concatenate([(query_t * SCALE).astype(BF16), attended_ref[t]], axis=0)
        out_ref[i * count : (i + 1) * count] = packed.T.reshape(count, cells, PAIR)

    run = keys // 4
    for i in range(len(plan) + 1):
        if i > 0:
            before_right = right
        if i < len(plan):
            cots, right, spread = load(*plan[i])
        for step in range(4):
            if i < len(plan):
                for block in range(step * sectors // 4, (step + 1) * sectors // 4, 2):
                    make_slopes(i, cots, spread, block)
            if i > 0:
                add_grads(i - 1, before_right, slice(step * run, (step + 1) * run))
        if i < len(plan):
            finish(i)


def merge_kernel(grad_ref, *refs):
    *part_refs, merged_ref = refs
    cells = grad_ref.shape[1]
    scale = lane_scale().reshape(1, 1, PAIR)
    for start, near_ref, far_ref in ((0, *part_refs[:2]), (part_refs[0].shape[0], *part_refs[2:4])):
        part = slice(start, start + near_ref.shape[0])
        grad = grad_ref[part] * scale + near_ref[...].astype(F32) + far_ref[...].astype(F32)
        merged_ref[part, cells:] = grad.astype(BF16)
    start = 0
    for out_ref in part_refs[4:]:
        merged_ref[start : start + out_ref.shape[0], :cells] = out_ref[...]
        start += out_ref.shape[0]


def unpack_kernel(merged_ref, attended_ref, query_ref, key_ref, value_ref):
    cells = attended_ref.shape[0]
    for head in range(0, HEADS, 2):
        lanes = slice(head * HEAD_DIM, (head + 2) * HEAD_DIM)
        for rows, first_ref, second_ref in (
            (slice(0, cells), query_ref, attended_ref),
            (slice(cells, 2 * cells), key_ref, value_ref),
        ):
            one, two = merged_ref[head, rows], merged_ref[head + 1, rows]
            first_ref[:, lanes] = jnp.concatenate([one[:, :HEAD_DIM], two[:, :HEAD_DIM]], axis=1)
            second_ref[:, lanes] = jnp.concatenate([one[:, HEAD_DIM:], two[:, HEAD_DIM:]], axis=1)


def cost(flops, nbytes):
    return pl.CostEstimate(flops=flops, bytes_accessed=nbytes, transcendentals=0)


def per_device(queries, key_vectors, value_vectors, cotangent, neighbour_lists, list_counts):
    _, band_rows, cycle_cols, features = queries.shape
    cells = band_rows * cycle_cols
    sectors = lax.axis_size("lon")
    bands = lax.axis_size("lat")
    part = sectors // 2
    steps = part // CHUNK
    wide = CHUNK * cells
    keys = sectors * cells
    flat = (cells, features)
    params = pltpu.CompilerParams(vmem_limit_bytes=24 * 1024 * 1024)
    struct = jax.ShapeDtypeStruct

    def both_ways(to_near, to_far):
        return lax.ppermute(to_near, "lat", near), lax.ppermute(to_far, "lat", far)

    def call(kernel, outs, args, name, flops, specs=None, scratch=(), compiler_params=params):
        return pl.pallas_call(
            kernel, out_shape=outs, in_specs=specs or [VMEM] * len(args),
            out_specs=(VMEM,) * len(outs), scratch_shapes=scratch,
            compiler_params=compiler_params, cost_estimate=cost(flops, 4 << 20), name=name,
        )(*args)

    packed = pl.pallas_call(
        pack_kernel, out_shape=struct((HEADS, 2 * cells, PAIR), BF16),
        in_specs=[ANY] * 4, out_specs=ANY,
        scratch_shapes=[
            pltpu.VMEM((4,) + flat, BF16), pltpu.VMEM((2, HEADS, cells, PAIR), BF16),
            pltpu.SemaphoreType.DMA((4,)), pltpu.SemaphoreType.DMA((2,)),
        ],
        cost_estimate=cost(0, 2 << 20), name="pack",
    )(*(a.reshape(flat) for a in (key_vectors, value_vectors, queries, cotangent)))
    (bias,) = call(
        bias_kernel, (struct((sectors + 2, keys), F32),), (neighbour_lists, list_counts),
        "bias", 10**8, [SMEM] * 2,
    )
    x = lax.all_to_all(packed, "lon", 0, 0, tiled=True)
    near = [(band, band ^ 1) for band in range(bands)]
    far = [(band, ((band + 1) ^ 1) - 1) for band in range(1, bands - 1)]
    far += [(0, bands - 1), (bands - 1, 0)]

    row = struct((steps, 1, wide), F32)
    tall = struct((steps, HEAD_DIM, wide), F32)
    tall_low = struct(tall.shape, BF16)
    by_part = struct((part, cells, PAIR), BF16)
    ahead = (struct((steps, keys, wide), BF16), row, row, tall)
    scores = [pltpu.VMEM((steps, keys, wide), F32)]

    kv = x[:part, :cells]
    rims = [both_ways(kv, kv)]
    weights, *stats, kv_t, kv = call(
        first_forward_kernel, ahead + (struct((PAIR, keys), BF16), by_part), (x, bias),
        "forward", 5 * 10**9, scratch=scores,
    )
    forward = [(weights, stats)]
    rims.append(both_ways(kv, kv))
    weights, *stats = call(
        functools.partial(forward_part, steps), ahead, (x, bias, kv_t), "forward", 5 * 10**9,
        scratch=scores,
    )
    forward.append((weights, stats))
    last = stats[0]
    groups, returned, outs, grad = (), (), (), ()
    for i, (weights, stats) in enumerate(forward):
        *for_queries, near_grad, far_grad = call(
            functools.partial(rims_kernel, i * steps),
            (tall_low, tall_low, row, tall, by_part, by_part),
            (x, bias) + rims[i] + tuple(stats) + (last,), "rims", 10**9,
        )
        returned += both_ways(near_grad, far_grad)
        groups += (weights, *for_queries)
        for plan in PLANS[i]:
            out, grad = call(
                functools.partial(backward_kernel, plan, steps),
                (
                    struct((len(plan) * CHUNK, cells, PAIR), BF16),
                    struct((sectors, cells, PAIR), F32),
                ),
                (x, kv_t) + groups + grad, "backward", 10**8,
                scratch=[pltpu.VMEM((2, keys, wide), BF16)],
            )
            grad = (grad,)
            outs += (out,)
        last = out
    (merged,) = call(
        merge_kernel, (struct((sectors, 2 * cells, PAIR), BF16),), grad + returned + outs,
        "merge", 0,
    )
    merged = lax.all_to_all(merged, "lon", 0, 0, tiled=True)
    results = call(unpack_kernel, (struct(flat, BF16),) * 4, (merged,), "unpack", 0)
    return tuple(result.reshape(queries.shape) for result in results)


def solution(mesh):
    blocks = P(None, "lat", "lon", None)
    return jax.shard_map(
        per_device, mesh=mesh, in_specs=(blocks,) * 4 + (P(), P()), out_specs=(blocks,) * 4,
        check_vma=False,
    )
```

```python
import functools

import jax
import jax.numpy as jnp
from jax import lax
from jax.experimental import pallas as pl
from jax.experimental.pallas import tpu as pltpu
from jax.sharding import PartitionSpec as P

HEADS = 16
HEAD_DIM = 64
PAIR = 2 * HEAD_DIM
SCALE = HEAD_DIM ** (-0.5)
LOG2E = 1.4426950408889634
MASKED = -1e30
CHUNK = 4
PLANS = ((((0, 0),),), (((0, 1), (1, 0), (1, 1)),))
BF16 = jnp.bfloat16
F32 = jnp.float32
NN = (((1,), (0,)), ((), ()))
NT = (((1,), (1,)), ((), ()))
VMEM = pl.BlockSpec(memory_space=pltpu.VMEM)
SMEM = pl.BlockSpec(memory_space=pltpu.SMEM)
ANY = pl.BlockSpec(memory_space=pl.ANY)


def dot(a, b, dims=NN):
    return lax.dot_general(a, b, dims, preferred_element_type=F32)


def pack_pairs(first_ref, second_ref, out_ref):
    for head in range(HEADS):
        lanes = slice(head * HEAD_DIM, (head + 1) * HEAD_DIM)
        out_ref[head] = jnp.concatenate([first_ref[:, lanes], second_ref[:, lanes]], axis=1)


def pack_kernel(key_ref, value_ref, query_ref, cot_ref, packed_ref, held, pairs, in_sems, out_sems):
    cells = key_ref.shape[0]
    arrivals = [
        pltpu.make_async_copy(ref, held.at[i], in_sems.at[i])
        for i, ref in enumerate((key_ref, value_ref, query_ref, cot_ref))
    ]
    for arrival in arrivals:
        arrival.start()
    departures = []
    for i in range(2):
        arrivals[2 * i].wait()
        arrivals[2 * i + 1].wait()
        rows = pl.ds(i * cells, cells)
        pack_pairs(held.at[2 * i], held.at[2 * i + 1], pairs.at[i])
        departures.append(
            pltpu.make_async_copy(pairs.at[i], packed_ref.at[:, rows], out_sems.at[i])
        )
        departures[i].start()
    for departure in departures:
        departure.wait()


def bias_kernel(lists_ref, counts_ref, bias_ref):
    band = lax.axis_index("lat")
    bands, slots = lists_ref.shape
    sectors = bias_ref.shape[0] - 2
    shape = (sectors, bias_ref.shape[1])
    cells = shape[1] // sectors
    key_sector = lax.broadcasted_iota(jnp.int32, shape, 0)
    query_sector = lax.broadcasted_iota(jnp.int32, shape, 1) // cells
    offset = key_sector - query_sector
    offset = jnp.where(offset < 0, offset + sectors, offset)
    count = counts_ref[band]
    bias = jnp.full(shape, MASKED, F32)
    for slot in range(slots):
        named = jnp.where(slot < count, lists_ref[band, slot], -1)
        bias = jnp.where(offset == named, 0.0, bias)
    bias_ref[:sectors] = bias
    outer = jnp.where((band > 0) & (band < bands - 1), 0.0, MASKED).astype(F32)
    row = lax.broadcasted_iota(jnp.int32, (2, shape[1]), 0)
    bias_ref[sectors:] = jnp.where(row == 0, 0.0, outer)


def lane_scale():
    lane = lax.broadcasted_iota(jnp.int32, (1, PAIR), 1)
    return jnp.where(lane < HEAD_DIM, SCALE, 1.0).astype(F32)


def fold_rows(values, combine):
    return combine(values.reshape(values.shape[0] // 8, 8, values.shape[1]), axis=0)


def forward_part(
    start, x_ref, bias_ref, kv_t_ref, weights_ref, highest_ref, total_ref, out_ref, scores,
    transpose=False,
):
    sectors, both, _ = x_ref.shape
    cells = both // 2
    chunks, keys, wide = weights_ref.shape
    count = wide // cells
    blocks = [slice(block * cells, (block + 2) * cells) for block in range(0, sectors, 2)]

    def score(t, queries, rows, highest):
        block = rows.start // cells
        lanes = slice((start + t) * wide, (start + t + 1) * wide)
        s = dot(x_ref[block : block + 2, :cells].reshape(2 * cells, PAIR), queries, NT)
        s = s.reshape(2, cells, wide) + bias_ref[block : block + 2, lanes].reshape(2, 1, wide)
        s = s.reshape(2 * cells, wide)
        scores[t, rows, :] = s
        return jnp.maximum(highest, fold_rows(s, jnp.max))

    lane = lax.broadcasted_iota(jnp.int32, (1, PAIR), 1)
    highest = total = None
    for t in range(chunks + 1):
        before, before_highest = t - 1, highest
        if t < chunks:
            qc = x_ref[(start + t) * count : (start + t + 1) * count, cells:].reshape(wide, PAIR)
            queries = jnp.where(lane < HEAD_DIM, qc, jnp.zeros_like(qc))
            highest = jnp.full((8, wide), -jnp.inf, F32)
        total = jnp.zeros((8, wide), F32)
        for rows in blocks:
            if t < chunks:
                highest = score(t, queries, rows, highest)
            if t == 0 and transpose:
                block = rows.start // cells
                pairs = x_ref[block : block + 2, :cells].reshape(2 * cells, PAIR)
                kv_t_ref[:, rows] = pairs.T
            if t > 0:
                p = jnp.exp2((scores[before, rows, :] - before_highest) * (SCALE * LOG2E))
                total = total + fold_rows(p, jnp.sum)
                weights_ref[before, rows, :] = p.astype(BF16)
        if t > 0:
            highest_ref[before] = before_highest
            total_ref[before] = jnp.sum(total, axis=0, keepdims=True)
            out_ref[before] = dot(kv_t_ref[HEAD_DIM:, :], weights_ref[before])
        highest = jnp.max(highest, axis=0, keepdims=True)


def first_forward_kernel(x_ref, bias_ref, *refs):
    *outs, kv_t_ref, kv_ref, scores = refs
    cells = kv_ref.shape[1]
    kv_ref[...] = x_ref[kv_ref.shape[0] :, :cells]
    forward_part(0, x_ref, bias_ref, kv_t_ref, *outs, scores, transpose=True)


def rims_kernel(
    start, x_ref, bias_ref, near_ref, far_ref, highest_ref, total_ref, out_ref, _,
    attended_ref, cot_ref, spread_ref, query_ref, near_grad_ref, far_grad_ref,
):
    sectors, both, _ = x_ref.shape
    cells = both // 2
    chunks, _, narrow = out_ref.shape
    wide = chunks * narrow
    count = wide // cells
    parts = [slice(a * cells, (a + 1) * cells) for a in range(count)]
    first = start * (narrow // cells)

    def beside(values):
        return jnp.concatenate(values, axis=1)

    def read(ref):
        return beside([ref[t] for t in range(chunks)])

    def write(ref, value):
        for t in range(chunks):
            ref[t] = value[:, t * narrow : (t + 1) * narrow]

    qc_t = x_ref[first : first + count, cells:].reshape(wide, PAIR).T
    zeros = jnp.zeros((HEAD_DIM, wide), BF16)
    queries = jnp.concatenate([qc_t[:HEAD_DIM], zeros], axis=0)
    rims = [jnp.concatenate([near_ref[a], far_ref[a]], axis=0) for a in range(count)]
    rims_t = [rim.T for rim in rims]
    bias = bias_ref[sectors : sectors + 2, first * cells : (first + count) * cells]
    s = beside([dot(rim, queries[:, part]) for rim, part in zip(rims, parts)])
    s = (s.reshape(2, cells, wide) + bias.reshape(2, 1, wide)).reshape(2 * cells, wide)
    own = read(highest_ref)
    highest = jnp.maximum(own, jnp.max(fold_rows(s, jnp.max), axis=0, keepdims=True))
    p = jnp.exp2((s - highest) * (SCALE * LOG2E))
    p_low = p.astype(BF16)
    ratio = jnp.exp2((own - highest) * (SCALE * LOG2E))
    total = ratio * read(total_ref) + jnp.sum(fold_rows(p, jnp.sum), axis=0, keepdims=True)
    inverse = 1.0 / total
    rim_out = [dot(rim_t[HEAD_DIM:], p_low[:, part]) for rim_t, part in zip(rims_t, parts)]
    out_t = read(out_ref) * ratio + beside(rim_out)
    attended = (out_t * inverse).astype(BF16)
    write(attended_ref, attended)
    cot_t = qc_t[HEAD_DIM:].astype(F32) * inverse
    own_cot = (cot_t * ratio).astype(BF16)
    write(cot_ref, own_cot)
    own_spread = own_cot.astype(F32) * attended.astype(F32)
    write(spread_ref, jnp.sum(own_spread, axis=0, keepdims=True))
    cot_t = cot_t.astype(BF16)
    spread = jnp.sum(cot_t.astype(F32) * attended.astype(F32), axis=0, keepdims=True)
    cots = jnp.concatenate([zeros, cot_t], axis=0)
    product = beside([dot(rim, cots[:, part]) for rim, part in zip(rims, parts)])
    slopes = (p * (product - spread)).astype(BF16)
    for a, part in enumerate(parts):
        left = beside([p_low[:, part], slopes[:, part]])
        right = beside([cots[:, part], queries[:, part]])
        grad = dot(left, right, NT) * lane_scale()
        near_grad_ref[a] = grad[:cells].astype(BF16)
        far_grad_ref[a] = grad[cells:].astype(BF16)
    query_t = [dot(rim_t[:HEAD_DIM], slopes[:, part]) for rim_t, part in zip(rims_t, parts)]
    write(query_ref, beside(query_t))


def backward_kernel(plan, steps, x_ref, kv_t_ref, *refs):
    parts = 1 + max(part for part, _ in plan)
    groups = [refs[5 * i : 5 * i + 5] for i in range(parts)]
    *before, out_ref, grad_ref, slopes_scr = refs[5 * parts :]
    sectors, both, _ = x_ref.shape
    cells = both // 2
    _, keys, wide = slopes_scr.shape
    count = wide // cells
    grad_ref[...] = before[0][...] if before else jnp.zeros_like(grad_ref)
    zeros = jnp.zeros((HEAD_DIM, wide), BF16)

    def load(part, t):
        first = (part * steps + t) * count
        queries_t = x_ref[first : first + count, cells:].reshape(wide, PAIR).T[:HEAD_DIM]
        queries = jnp.concatenate([queries_t, zeros], axis=0)
        cots = jnp.concatenate([zeros, groups[part][2][t]], axis=0)
        return cots, jnp.concatenate([cots, queries], axis=1), groups[part][3][t]

    def make_slopes(i, cots, spread, block):
        part, t = plan[i]
        rows = slice(block * cells, (block + 2) * cells)
        product = dot(x_ref[block : block + 2, :cells].reshape(2 * cells, PAIR), cots)
        slopes = groups[part][0][t, rows, :].astype(F32) * (product - spread)
        slopes_scr[i % 2, rows, :] = slopes.astype(BF16)

    def add_grads(i, right, rows):
        part, t = plan[i]
        left = jnp.concatenate([groups[part][0][t, rows, :], slopes_scr[i % 2, rows, :]], axis=1)
        first, last = rows.start // cells, rows.stop // cells
        grad_ref[first:last] += dot(left, right, NT).reshape(last - first, cells, PAIR)

    def finish(i):
        part, t = plan[i]
        attended_ref, query_ref = groups[part][1], groups[part][4]
        query_t = query_ref[t] + dot(kv_t_ref[:HEAD_DIM, :], slopes_scr[i % 2])
        packed = jnp.concatenate([(query_t * SCALE).astype(BF16), attended_ref[t]], axis=0)
        out_ref[i * count : (i + 1) * count] = packed.T.reshape(count, cells, PAIR)

    run = keys // 4
    for i in range(len(plan) + 1):
        if i > 0:
            before_right = right
        if i < len(plan):
            cots, right, spread = load(*plan[i])
        for step in range(4):
            if i < len(plan):
                for block in range(step * sectors // 4, (step + 1) * sectors // 4, 2):
                    make_slopes(i, cots, spread, block)
            if i > 0:
                add_grads(i - 1, before_right, slice(step * run, (step + 1) * run))
        if i < len(plan):
            finish(i)


def merge_kernel(grad_ref, *refs):
    *part_refs, merged_ref = refs
    cells = grad_ref.shape[1]
    scale = lane_scale().reshape(1, 1, PAIR)
    for start, near_ref, far_ref in ((0, *part_refs[:2]), (part_refs[0].shape[0], *part_refs[2:4])):
        part = slice(start, start + near_ref.shape[0])
        grad = grad_ref[part] * scale + near_ref[...].astype(F32) + far_ref[...].astype(F32)
        merged_ref[part, cells:] = grad.astype(BF16)
    start = 0
    for out_ref in part_refs[4:]:
        merged_ref[start : start + out_ref.shape[0], :cells] = out_ref[...]
        start += out_ref.shape[0]


def unpack_kernel(merged_ref, attended_ref, query_ref, key_ref, value_ref, held, sems):
    cells = attended_ref.shape[0]
    copies = []
    for i, (first_ref, second_ref) in enumerate(((query_ref, attended_ref), (key_ref, value_ref))):
        rows = slice(i * cells, (i + 1) * cells)
        for head in range(0, HEADS, 2):
            lanes = slice(head * HEAD_DIM, (head + 2) * HEAD_DIM)
            one, two = merged_ref[head, rows], merged_ref[head + 1, rows]
            held[2 * i, :, lanes] = jnp.concatenate([one[:, :HEAD_DIM], two[:, :HEAD_DIM]], axis=1)
            held[2 * i + 1, :, lanes] = jnp.concatenate(
                [one[:, HEAD_DIM:], two[:, HEAD_DIM:]], axis=1
            )
        for j, ref in ((2 * i, first_ref), (2 * i + 1, second_ref)):
            copies.append(pltpu.make_async_copy(held.at[j], ref, sems.at[j]))
            copies[j].start()
    for copy in copies:
        copy.wait()


def cost(flops, nbytes):
    return pl.CostEstimate(flops=flops, bytes_accessed=nbytes, transcendentals=0)


def per_device(queries, key_vectors, value_vectors, cotangent, neighbour_lists, list_counts):
    _, band_rows, cycle_cols, features = queries.shape
    cells = band_rows * cycle_cols
    sectors = lax.axis_size("lon")
    bands = lax.axis_size("lat")
    part = sectors // 2
    steps = part // CHUNK
    wide = CHUNK * cells
    keys = sectors * cells
    flat = (cells, features)
    params = pltpu.CompilerParams(vmem_limit_bytes=24 * 1024 * 1024)
    struct = jax.ShapeDtypeStruct

    def both_ways(to_near, to_far):
        return lax.ppermute(to_near, "lat", near), lax.ppermute(to_far, "lat", far)

    def call(kernel, outs, args, name, flops, specs=None, scratch=(), compiler_params=params):
        return pl.pallas_call(
            kernel, out_shape=outs, in_specs=specs or [VMEM] * len(args),
            out_specs=(VMEM,) * len(outs), scratch_shapes=scratch,
            compiler_params=compiler_params, cost_estimate=cost(flops, 4 << 20), name=name,
        )(*args)

    packed = pl.pallas_call(
        pack_kernel, out_shape=struct((HEADS, 2 * cells, PAIR), BF16),
        in_specs=[ANY] * 4, out_specs=ANY,
        scratch_shapes=[
            pltpu.VMEM((4,) + flat, BF16), pltpu.VMEM((2, HEADS, cells, PAIR), BF16),
            pltpu.SemaphoreType.DMA((4,)), pltpu.SemaphoreType.DMA((2,)),
        ],
        cost_estimate=cost(0, 2 << 20), name="pack",
    )(*(a.reshape(flat) for a in (key_vectors, value_vectors, queries, cotangent)))
    (bias,) = call(
        bias_kernel, (struct((sectors + 2, keys), F32),), (neighbour_lists, list_counts),
        "bias", 10**8, [SMEM] * 2,
    )
    x = lax.all_to_all(packed, "lon", 0, 0, tiled=True)
    near = [(band, band ^ 1) for band in range(bands)]
    far = [(band, ((band + 1) ^ 1) - 1) for band in range(1, bands - 1)]
    far += [(0, bands - 1), (bands - 1, 0)]

    row = struct((steps, 1, wide), F32)
    tall = struct((steps, HEAD_DIM, wide), F32)
    tall_low = struct(tall.shape, BF16)
    by_part = struct((part, cells, PAIR), BF16)
    ahead = (struct((steps, keys, wide), BF16), row, row, tall)
    scores = [pltpu.VMEM((steps, keys, wide), F32)]

    kv = x[:part, :cells]
    rims = [both_ways(kv, kv)]
    weights, *stats, kv_t, kv = call(
        first_forward_kernel, ahead + (struct((PAIR, keys), BF16), by_part), (x, bias),
        "forward", 5 * 10**9, scratch=scores,
    )
    forward = [(weights, stats)]
    rims.append(both_ways(kv, kv))
    weights, *stats = call(
        functools.partial(forward_part, steps), ahead, (x, bias, kv_t), "forward", 5 * 10**9,
        scratch=scores,
    )
    forward.append((weights, stats))
    last = stats[0]
    groups, returned, outs, grad = (), (), (), ()
    for i, (weights, stats) in enumerate(forward):
        *for_queries, near_grad, far_grad = call(
            functools.partial(rims_kernel, i * steps),
            (tall_low, tall_low, row, tall, by_part, by_part),
            (x, bias) + rims[i] + tuple(stats) + (last,), "rims", 10**9,
        )
        returned += both_ways(near_grad, far_grad)
        groups += (weights, *for_queries)
        for plan in PLANS[i]:
            out, grad = call(
                functools.partial(backward_kernel, plan, steps),
                (
                    struct((len(plan) * CHUNK, cells, PAIR), BF16),
                    struct((sectors, cells, PAIR), F32),
                ),
                (x, kv_t) + groups + grad, "backward", 10**8,
                scratch=[pltpu.VMEM((2, keys, wide), BF16)],
            )
            grad = (grad,)
            outs += (out,)
        last = out
    (merged,) = call(
        merge_kernel, (struct((sectors, 2 * cells, PAIR), BF16),), grad + returned + outs,
        "merge", 0,
    )
    merged = lax.all_to_all(merged, "lon", 0, 0, tiled=True)
    results = pl.pallas_call(
        unpack_kernel, out_shape=(struct(flat, BF16),) * 4, in_specs=[VMEM], out_specs=(ANY,) * 4,
        scratch_shapes=[pltpu.VMEM((4,) + flat, BF16), pltpu.SemaphoreType.DMA((4,))],
        compiler_params=params, cost_estimate=cost(0, 2 << 20), name="unpack",
    )(merged)
    return tuple(result.reshape(queries.shape) for result in results)


def solution(mesh):
    blocks = P(None, "lat", "lon", None)
    return jax.shard_map(
        per_device, mesh=mesh, in_specs=(blocks,) * 4 + (P(), P()), out_specs=(blocks,) * 4,
        check_vma=False,
    )
```
